256 devices in a mesh: group: 2 (over core), tile: 128 (over z, x, y).
Axes of the slice: x: 4, y: 4, z: 8, core: 2. Of those that a mesh axis runs over, the one named last changes fastest.
Arguments:
- species_amounts: float32 [2, 220, 8, 16384], P('group', None, None, 'tile'), may hold values from 0.01 to 2
- air_warmth_kelvin: float32 [8, 16384], P(None, 'tile'), may hold values from 200 to 300
- sunlight_strength: float32 [8, 16384], P(None, 'tile'), may hold values from 0.1 to 1
- wind_stability_numbers: float32 [8, 16384], P(None, 'tile'), may hold values from -0.8 to 0.8
- illuminated_marker: int32 [16384], replicated, may hold values from 0 to 1, as said below
- position_vertical_lookup: int32 [16384], replicated, may hold values from 0 to 16383, as said below
- speed_constants: float32 [500], replicated, may hold values from 0.02 to 3
- barrier_kelvins: float32 [500], replicated, may hold values from 0 to 1200
- consumed_species: int32 [2, 500], replicated, may hold values from 0 to 219, as said below
- outcome_species: int32 [2, 500], replicated, may hold values from 0 to 219
- outcome_fractions: float32 [2, 500], replicated, may hold values from 0.3 to 1
Outputs:
- state: float32 [2, 220, 8, 16384], P('group', None, None, 'tile')
The draws below stay inside these ranges and needn't reach their ends.
Inputs may be any that keep to these rules, and one draw needn't show every extreme that they name: `illuminated_marker`: 1 exactly on the columns of 64 consecutive tiles of 128 columns, counted cyclically along the slab from a random tile. `position_vertical_lookup`: A permutation of the columns; slot o * 128 + s + j, for j below 1, holds a column of tile s. `consumed_species`: the two reactants of a reaction differ; the second is not read for the first 64 reactions.
All inputs are finite; a program needn't handle non-finite values.
Results may differ from the reference program's by a relative error of at most 0.0003.
Values sent between devices are 32-bit elements; how exact they have to be, the bound alone decides.
No kernel may reach another device: no remote copies, remote signals or barrier semaphores. Data moves between devices by JAX's collectives and lax.ppermute only.
A program may use at most 64 MiB of HBM per device.

```python
import math
import jax
import jax.numpy as jnp
from jax import lax

SPEC = 220
REAC = 500
PHOT = 64
ALTITUDE_LAYERS = 8
PATCH_VERTICALS = 128
ADV_STEPS = 4
ITER_NIGHT = 2
ITER_DAY = 4
GRID_VERTICALS = 16384
PAIR = 1
DAY_TILES = 64
N_TILE = 128


def draw_consumed_species(key, part):
    key = jax.random.fold_in(key, 11)
    first_key, offset_key = jax.random.split(key)
    first = jax.random.randint(first_key, (REAC,), 0, SPEC)
    offset = jax.random.randint(offset_key, (REAC,), 1, SPEC)
    return jnp.stack([first, (first + offset) % SPEC]).astype(jnp.int32)


def draw_illuminated_marker(key, part):
    key = jax.random.fold_in(key, 12)
    tile_count = GRID_VERTICALS // PATCH_VERTICALS
    begin = jax.random.randint(key, (), 0, tile_count)
    tile_of = jnp.arange(GRID_VERTICALS, dtype=jnp.int32) // PATCH_VERTICALS
    return ((tile_of - begin) % tile_count < DAY_TILES).astype(jnp.int32)


def draw_position_vertical_lookup(key, part):
    key = jax.random.fold_in(key, 13)
    tile_count = GRID_VERTICALS // PATCH_VERTICALS
    keys = jax.random.split(key, tile_count)

    def shuffle(single_key):
        return jax.random.permutation(single_key, PATCH_VERTICALS)
    orders = jax.vmap(shuffle)(keys).astype(jnp.int32)
    arranged = jnp.transpose(orders.reshape(tile_count, tile_count, PAIR), (1, 0, 2))
    offsets = (jnp.arange(tile_count, dtype=jnp.int32) * PATCH_VERTICALS)[None, :, None]
    return (arranged + offsets).reshape(GRID_VERTICALS).astype(jnp.int32)


def set_ends(drawn, rng, low, high):
    dims = drawn.shape
    index_at = [jax.random.randint(jax.random.fold_in(rng, axis), (), 0, dims[axis]) for axis in range(len(dims))]
    drawn = drawn.at[tuple(index_at)].set(low)
    longest = dims.index(max(dims))
    index_at[longest] = (index_at[longest] + 1) % dims[longest]
    return drawn.at[tuple(index_at)].set(high)


def level_of(stream_key, shape, shards, smallest, largest):
    def one(dim, shards_of):
        draws = jax.random.uniform(jax.random.fold_in(jax.random.fold_in(stream_key, 6), dim), (shards_of,), jnp.float32, smallest / len(shards), largest / len(shards))
        return jnp.repeat(jnp.exp(draws), shape[dim] // shards_of).reshape((-1,) + (1,) * (len(shape) - dim - 1))

    gain = one(*shards[0])
    for cut in shards[1:]:
        gain = gain * one(*cut)
    return gain


def setup_inputs(seed: int = 0) -> dict:
    key_of = jax.random.split(jax.random.key(seed), 12)
    species_amounts = jnp.clip(jnp.exp(math.log(2.0) - 5.2983174 * jax.random.uniform(key_of[0], (2, SPEC, ALTITUDE_LAYERS, GRID_VERTICALS), jnp.float32) ** level_of(key_of[0], (2, SPEC, ALTITUDE_LAYERS, GRID_VERTICALS), ((0, 2), (3, 128)), -0.2, 0.2)), 0.01, 2.0)
    air_warmth_kelvin = jnp.clip(200.0 + 100.0 * jax.random.uniform(key_of[1], (ALTITUDE_LAYERS, GRID_VERTICALS), jnp.float32) ** level_of(key_of[1], (ALTITUDE_LAYERS, GRID_VERTICALS), ((1, 128),), -0.2, 0.2), 200.0, 300.0)
    sunlight_strength = jnp.clip(jnp.exp(math.log(1.0) - 2.3025851 * jax.random.uniform(key_of[2], (ALTITUDE_LAYERS, GRID_VERTICALS), jnp.float32) ** level_of(key_of[2], (ALTITUDE_LAYERS, GRID_VERTICALS), ((1, 128),), -0.2, 0.2)), 0.1, 1.0)
    wind_stability_numbers = jnp.clip(jax.random.uniform(key_of[3], (ALTITUDE_LAYERS, GRID_VERTICALS), jnp.float32, -0.8, 0.8) * level_of(key_of[3], (ALTITUDE_LAYERS, GRID_VERTICALS), ((1, 128),), -0.4, 0.0), -0.8, 0.8)
    illuminated_marker = draw_illuminated_marker(jax.random.fold_in(key_of[11], 71), 0)
    position_vertical_lookup = draw_position_vertical_lookup(jax.random.fold_in(key_of[11], 71), 0)
    speed_constants = jnp.clip(jnp.exp(jax.random.uniform(key_of[6], (REAC,), jnp.float32, math.log(0.02), math.log(3.0))), 0.02, 3.0)
    barrier_kelvins = jnp.clip(jax.random.uniform(key_of[7], (REAC,), jnp.float32, 0.0, 1200.0), 0.0, 1200.0)
    consumed_species = draw_consumed_species(jax.random.fold_in(key_of[11], 71), 0)
    outcome_species = set_ends(jax.random.randint(key_of[9], (2, REAC), 0, SPEC), jax.random.fold_in(key_of[9], 1), 0, SPEC - 1).astype(jnp.int32)
    outcome_fractions = jnp.clip(jax.random.uniform(key_of[10], (2, REAC), jnp.float32, 0.3, 1.0), 0.3, 1.0)
    return {"species_amounts": species_amounts, "air_warmth_kelvin": air_warmth_kelvin, "sunlight_strength": sunlight_strength, "wind_stability_numbers": wind_stability_numbers, "illuminated_marker": illuminated_marker, "position_vertical_lookup": position_vertical_lookup, "speed_constants": speed_constants, "barrier_kelvins": barrier_kelvins, "consumed_species": consumed_species, "outcome_species": outcome_species, "outcome_fractions": outcome_fractions}


def wendroff(left, middle, right, wind):
    return middle - 0.5 * wind * (right - left) + 0.5 * wind * wind * (right - 2.0 * middle + left)


def mechanism(consumed_species, outcome_species, outcome_fractions):
    species = jnp.arange(SPEC, dtype=jnp.int32)[:, None]
    light_splitting_speeds = jnp.arange(REAC, dtype=jnp.int32) < PHOT
    producing = outcome_fractions[0][None, :] * (outcome_species[0][None, :] == species) + outcome_fractions[1][None, :] * (outcome_species[1][None, :] == species)
    consuming = jnp.concatenate([consumed_species[0][None, :] == species, (consumed_species[1][None, :] == species) & jnp.logical_not(light_splitting_speeds)[None, :]], axis=1).astype(outcome_fractions.dtype)
    return producing, consuming, light_splitting_speeds


def reaction_speed_constants(air_warmth_kelvin, sunshine_strength, sunshine_markers, speed_constants, barrier_kelvins, light_splitting_speeds):
    warmth_driven_speeds = speed_constants[:, None, None] * jnp.exp(barrier_kelvins[:, None, None] * (1.0 / 250.0 - 1.0 / air_warmth_kelvin[None]))
    photo = speed_constants[:, None, None] * jnp.where(sunshine_markers[None, :] > 0, sunshine_strength, 0.0)[None]
    return jnp.where(light_splitting_speeds[:, None, None], photo, warmth_driven_speeds)


def sweep(concen, start, coefficient, tables, consumed_species):
    producing, consuming, light_splitting_speeds = tables
    first = jnp.take(concen, consumed_species[0], axis=0)
    second = jnp.where(light_splitting_speeds[:, None], 1.0, jnp.take(concen, consumed_species[1], axis=0))
    produced = jnp.dot(producing, coefficient * first * second, precision=lax.Precision.HIGHEST, preferred_element_type=jnp.float32)
    stacked = jnp.concatenate([coefficient * second, coefficient * first], axis=0)
    lost = jnp.dot(consuming, stacked, precision=lax.Precision.HIGHEST, preferred_element_type=jnp.float32)
    return (start + produced) / (1.0 + lost)


def solve(start3, concen3, coefficient3, count, tables, consumed_species):
    shape = concen3.shape
    start = start3.reshape(shape[0], -1)
    concen = concen3.reshape(shape[0], -1)
    coefficient = coefficient3.reshape(coefficient3.shape[0], -1)
    for sweep_index in range(count):
        concen = sweep(concen, start, coefficient, tables, consumed_species)
    return concen.reshape(shape)


def reference(species_amounts, air_warmth_kelvin, sunlight_strength, wind_stability_numbers, illuminated_marker, position_vertical_lookup, speed_constants, barrier_kelvins, consumed_species, outcome_species, outcome_fractions):
    tables = mechanism(consumed_species, outcome_species, outcome_fractions)
    advected = species_amounts[0]
    for step in range(ADV_STEPS):
        padded = jnp.pad(advected, ((0, 0), (0, 0), (1, 1)))
        advected = wendroff(padded[:, :, :-2], advected, padded[:, :, 2:], wind_stability_numbers)

    def patches_foremost_axis(array):
        return jnp.moveaxis(array.reshape(array.shape[:-1] + (N_TILE, PATCH_VERTICALS)), -2, 0)

    def patch_reaction_solver(block):
        earlier_species_amounts, temp_block, light_block, flag_block = block
        coefficient3 = reaction_speed_constants(temp_block, light_block, flag_block, speed_constants, barrier_kelvins, tables[2])
        night = solve(earlier_species_amounts, earlier_species_amounts, coefficient3, ITER_NIGHT, tables, consumed_species)
        day = solve(earlier_species_amounts, night, coefficient3, ITER_DAY - ITER_NIGHT, tables, consumed_species)
        return jnp.where(flag_block[None, None, :] > 0, day, night)

    patch_reaction_results = lax.map(patch_reaction_solver, (patches_foremost_axis(species_amounts[1]), patches_foremost_axis(air_warmth_kelvin), patches_foremost_axis(sunlight_strength), illuminated_marker.reshape(N_TILE, PATCH_VERTICALS)))
    chem = jnp.moveaxis(patch_reaction_results, 0, -2).reshape(species_amounts[1].shape)
    state_next = advected + (chem - species_amounts[1])
    owned = jnp.take(chem, position_vertical_lookup, axis=2)
    return jnp.stack([state_next, owned])
```

```python
import jax
import jax.numpy as jnp
from jax import lax
from jax.experimental import pallas as pl
from jax.experimental.pallas import tpu as pltpu
from jax.sharding import PartitionSpec as P

SPEC = 220
REAC = 500
PHOT = 64
LAYERS = 8
COLS = 128
ADV_STEPS = 4
ITER_NIGHT = 2
ITER_DAY = 4

HALF = LAYERS // 2
ROWS = SPEC * LAYERS
SPAD = 224
KDIM = 256
RPAD = 512
CELLS = HALF * COLS
CHUNK = 256
EDGE = 4
DARK = -1024.0

ORDER = [z * 16 + xy for z in (7, 3, 6, 2, 5, 1, 4, 0) for xy in range(15, -1, -1)]

VMEM = pl.BlockSpec(memory_space=pltpu.VMEM)
SMEM = pl.BlockSpec(memory_space=pltpu.SMEM)
ANY = pl.BlockSpec(memory_space=pl.ANY)
HBM = pl.BlockSpec(memory_space=pltpu.HBM)
PARAMS = pltpu.CompilerParams(vmem_limit_bytes=24 * 1024 * 1024)


def high_low(value):
    high = value.astype(jnp.bfloat16)
    return high, (value - high.astype(jnp.float32)).astype(jnp.bfloat16)


def dot(a, b):
    return jnp.dot(a, b, preferred_element_type=jnp.float32)


def tile_at(place):
    step = place // 16
    return (7 - step // 2 - 4 * (step % 2)) * 16 + 15 - place % 16


def place_of(tile):
    z = tile // 16
    return (2 * (3 - z % 4) + 1 - z // 4) * 16 + 15 - tile % 16


def prepare_kernel(
    tile_of,
    heat,
    light,
    consumed,
    outcome,
    fractions,
    speeds,
    barriers,
    weights,
    gather,
    terms,
    heat_here,
    light_here,
    consumed_here,
    outcome_here,
    fractions_here,
    speeds_here,
    barriers_here,
    turning,
    sems,
):
    group = tile_of[0]
    copies = [
        pltpu.make_async_copy(source, target, sems.at[place])
        for place, (source, target) in enumerate(
            (
                (consumed, consumed_here),
                (outcome, outcome_here),
                (fractions, fractions_here),
                (speeds, speeds_here),
                (barriers, barriers_here),
                (heat, heat_here),
                (light, light_here),
            )
        )
    ]
    for copy in copies:
        copy.start()
    spare = pl.ds(RPAD - COLS, COLS)
    weights[:, spare] = jnp.zeros((3 * SPAD, COLS), jnp.bfloat16)
    turning[:, spare] = jnp.zeros((KDIM, COLS), jnp.float32)
    for copy in copies:
        copy.wait()

    used = pl.ds(0, REAC)
    species = lax.broadcasted_iota(jnp.int32, (SPAD, REAC), 0)
    thermal = lax.broadcasted_iota(jnp.int32, (1, REAC), 1) >= PHOT
    second = jnp.where(thermal, consumed_here[1:2, :], -1)
    consuming = jnp.where(species == consumed_here[0:1, :], 1.0, 0.0) + jnp.where(
        species == second, 1.0, 0.0
    )
    producing = jnp.where(species == outcome_here[0:1, :], fractions_here[0:1, :], 0.0) + jnp.where(
        species == outcome_here[1:2, :], fractions_here[1:2, :], 0.0
    )
    producing_high, producing_low = high_low(producing)
    weights[pl.ds(0, SPAD), used] = consuming.astype(jnp.bfloat16)
    weights[pl.ds(SPAD, SPAD), used] = producing_high
    weights[pl.ds(2 * SPAD, SPAD), used] = producing_low

    speed = lax.log2(speeds_here[...])
    speed_high = speed.astype(jnp.bfloat16).astype(jnp.float32)
    speed_mid = (speed - speed_high).astype(jnp.bfloat16).astype(jnp.float32)
    speed_low = speed - speed_high - speed_mid
    barrier = jnp.where(thermal, barriers_here[...], 0.0)
    barrier_high = barrier.astype(jnp.bfloat16).astype(jnp.float32)
    barrier_low = barrier - barrier_high
    photo = jnp.where(thermal, 0.0, 1.0)
    row = lax.broadcasted_iota(jnp.int32, (KDIM - SPAD, REAC), 0)
    extra = jnp.zeros((KDIM - SPAD, REAC), jnp.float32)
    for place, value in enumerate(
        (barrier_high, barrier_low, speed_high, speed_mid, speed_low, photo)
    ):
        extra = jnp.where(row == place, value, extra)
    turning[pl.ds(0, SPAD), used] = consuming
    turning[pl.ds(SPAD, KDIM - SPAD), used] = extra
    gather[...] = jnp.transpose(turning[...]).astype(jnp.bfloat16)

    row = lax.broadcasted_iota(jnp.int32, (KDIM - SPAD, COLS), 0)
    for layer in range(HALF):
        warmth = heat_here[pl.ds(group * HALF + layer, 1), :]
        flux = light_here[pl.ds(group * HALF + layer, 1), :]
        inverse = (1.0 / 250.0 - 1.0 / warmth) * 1.4426950408889634
        term = jnp.where(row < 2, inverse, 0.0)
        term = jnp.where((row >= 2) & (row < 5), 1.0, term)
        term = jnp.where(row == 5, lax.log2(flux), term)
        term_high, term_low = high_low(term)
        terms[0 : KDIM - SPAD, pl.ds(layer * COLS, COLS)] = term_high
        terms[KDIM - SPAD : 2 * (KDIM - SPAD), pl.ds(layer * COLS, COLS)] = term_low


def chemistry_kernel(
    tile_of,
    own,
    swapped,
    marker,
    lookup,
    weights,
    gather,
    terms,
    send,
    tendency,
    amounts,
    logs,
    start,
    now,
    sem,
):
    group, tile = tile_of[0], tile_of[1]

    @pl.when(group == 1)
    def _():
        pltpu.make_async_copy(own, amounts.at[pl.ds(0, ROWS)], sem).start()

    @pl.when(group == 0)
    def _():
        pltpu.make_async_copy(swapped, amounts.at[pl.ds(0, ROWS)], sem).start()

    lit = jnp.max(marker[pl.ds(tile, 1), :])
    sweeps = jnp.where(lit > 0, ITER_DAY, ITER_NIGHT)
    extra = KDIM - SPAD
    dark = (lax.broadcasted_iota(jnp.int32, (extra, CELLS), 0) == 5) & (lit <= 0)
    for place, value in ((SPAD, DARK), (KDIM + SPAD, 0.0)):
        term = terms[pl.ds(0 if place == SPAD else extra, extra), :].astype(jnp.float32)
        logs[pl.ds(place, extra), :] = jnp.where(dark, value, term).astype(jnp.bfloat16)
    amounts[pl.ds(ROWS, SPAD * LAYERS - ROWS), :] = jnp.ones(
        (SPAD * LAYERS - ROWS, COLS), jnp.float32
    )
    pltpu.make_async_copy(own, amounts.at[pl.ds(0, ROWS)], sem).wait()
    for layer in range(HALF):
        begin = amounts[pl.ds(group * HALF + layer, SPAD, stride=LAYERS), :]
        start[:, pl.ds(layer * COLS, COLS)] = begin
        now[:, pl.ds(layer * COLS, COLS)] = begin

    chunks = [pl.ds(at, CHUNK) for at in range(0, CELLS, CHUNK)]

    @pl.loop(0, sweeps)
    def _(_):
        for cells in chunks:
            log_high, log_low = high_low(lax.log2(now[:, cells]))
            logs[0:SPAD, cells] = log_high
            logs[KDIM : KDIM + SPAD, cells] = log_low
        for cells in chunks:
            rate = jnp.exp2(
                dot(gather[...], logs[0:KDIM, cells]) + dot(gather[...], logs[KDIM:, cells])
            )
            high, low = high_low(rate)
            both = dot(weights[0 : 2 * SPAD], high) + dot(weights[0 : 2 * SPAD], low)
            gain = both[SPAD:] + dot(weights[2 * SPAD :], high)
            concen = now[:, cells]
            now[:, cells] = concen * (start[:, cells] + gain) / (concen + both[:SPAD])

    lane = lax.broadcasted_iota(jnp.int32, (COLS, COLS), 1)
    column = jnp.sum(jnp.where(lane == tile, lookup[...], 0), axis=1, keepdims=True)
    pick = jnp.where(lane == column - tile * COLS, 1.0, 0.0)
    ordered = jnp.where(lane == tile_at(lax.broadcasted_iota(jnp.int32, (COLS, COLS), 0)), 1.0, 0.0)
    choose = dot(ordered.astype(jnp.bfloat16), pick.astype(jnp.bfloat16)).astype(jnp.bfloat16)
    for layer in range(HALF):
        cells = pl.ds(layer * COLS, COLS)
        solved = now[:, cells]
        tendency[pl.ds(layer * SPAD, SPAD), :] = solved - start[:, cells]
        rest = jnp.concatenate([solved, jnp.zeros((KDIM - SPAD, COLS), jnp.float32)], axis=0)
        parts = []
        for _ in range(3):
            part = rest.astype(jnp.bfloat16)
            rest = rest - part.astype(jnp.float32)
            parts.append(across(choose, part))
        turned = parts[0] + parts[1] + parts[2]
        for half in range(2):
            send[pl.ds(2 * layer + half, COLS, stride=LAYERS), :] = turned[
                :, half * COLS : (half + 1) * COLS
            ]


def across(a, b):
    return lax.dot_general(a, b, (((1,), (1,)), ((), ())), preferred_element_type=jnp.float32)


def edge_kernel(tracers, wind, packed, padded):
    row = lax.broadcasted_iota(jnp.int32, (2 * EDGE, COLS), 0)
    column = lax.broadcasted_iota(jnp.int32, (2 * EDGE, COLS), 1)
    pick = jnp.where(column == (row + COLS - EDGE) % COLS, 1.0, 0.0).astype(jnp.bfloat16)
    for layer in range(LAYERS):
        padded[layer, SPEC - 4 :, :] = jnp.zeros((KDIM - SPEC + 4, COLS), jnp.float32)
        padded[layer, 0:SPEC, :] = tracers[pl.ds(layer, SPEC, stride=LAYERS), :]
        padded[layer, SPEC : SPEC + 1, :] = wind[layer : layer + 1, :]
    for layer in range(LAYERS):
        high, low = high_low(padded[layer])
        packed[pl.ds(layer * 2 * EDGE, 2 * EDGE), :] = across(pick, high) + across(pick, low)


def advect(tile, tracers, wind, from_low, from_high, own_tend, other_tend, state):
    sides = 2 * EDGE * LAYERS
    low_part = lax.broadcasted_iota(jnp.int32, (sides, KDIM), 0) % (2 * EDGE) < EDGE
    low_there = jnp.where(tile > 0, 1.0, 0.0)
    high_there = jnp.where(tile < COLS - 1, 1.0, 0.0)
    beside = jnp.where(low_part, from_low[...] * low_there, from_high[...] * high_there)
    beside = jnp.concatenate([beside, jnp.zeros((COLS - sides, KDIM), jnp.float32)], axis=0)
    beside = jnp.transpose(beside)
    wind_row = jnp.broadcast_to(beside[SPEC : SPEC + 1, :], (LAYERS, COLS))
    layer_of = lax.broadcasted_iota(jnp.int32, (LAYERS, COLS), 0)
    wind_side = jnp.zeros((LAYERS, COLS), jnp.float32)
    for layer in range(LAYERS):
        moved = pltpu.roll(wind_row, (COLS - EDGE - 2 * EDGE * layer) % COLS, 1)
        wind_side = jnp.where(layer_of == layer, moved, wind_side)

    lane = lax.broadcasted_iota(jnp.int32, (LAYERS, COLS), 1)
    lowest, highest = lane == 0, lane == COLS - 1

    def left(pair):
        up = [pltpu.roll(v, 1, 1) for v in pair]
        return jnp.where(lowest, up[1], up[0]), jnp.where(lowest, up[0], up[1])

    def right(pair):
        down = [pltpu.roll(v, COLS - 1, 1) for v in pair]
        return jnp.where(highest, down[1], down[0]), jnp.where(highest, down[0], down[1])

    factors = [
        (0.5 * c * (1.0 + c), 1.0 - c * c, 0.5 * c * (c - 1.0)) for c in (wind[...], wind_side)
    ]
    one = jnp.ones((LAYERS, COLS), jnp.float32)
    band = {0: (one, one)}
    for _ in range(ADV_STEPS):
        lefts = {d: left(pair) for d, pair in band.items()}
        rights = {d: right(pair) for d, pair in band.items()}
        reach = max(band) + 1
        fresh = {}
        for d in range(-reach, reach + 1):
            total = [0.0, 0.0]
            for source, factor in ((lefts.get(d + 1), 0), (band.get(d), 1), (rights.get(d - 1), 2)):
                if source is not None:
                    total = [t + factors[i][factor] * source[i] for i, t in enumerate(total)]
            fresh[d] = tuple(total)
        band = fresh

    rows = lax.broadcasted_iota(jnp.int32, (KDIM, COLS), 0)
    extra = rows - COLS
    edge = extra % (2 * EDGE)
    place = jnp.where(rows < COLS, rows, jnp.where(edge < EDGE, edge - EDGE, edge - EDGE + COLS))
    offset = place - lax.broadcasted_iota(jnp.int32, (KDIM, COLS), 1)
    beside_high, beside_low = high_low(beside[:SPAD])
    for layer in range(LAYERS):
        here = (rows < COLS) | (extra // (2 * EDGE) == layer)
        matrix = jnp.zeros((KDIM, COLS), jnp.float32)
        for d, (weight, _) in band.items():
            matrix = jnp.where(offset == d, weight[layer : layer + 1, :], matrix)
        matrix_high, matrix_low = high_low(jnp.where(here, matrix, 0.0))
        main = jnp.concatenate(
            [
                tracers[pl.ds(layer, SPEC, stride=LAYERS), :],
                jnp.zeros((SPAD - SPEC, COLS), jnp.float32),
            ],
            axis=0,
        )
        main_high, main_low = high_low(main)
        high = jnp.concatenate([main_high, beside_high], axis=1)
        low = jnp.concatenate([main_low, beside_low], axis=1)
        moved = dot(high, matrix_high) + dot(low, matrix_high) + dot(high, matrix_low)
        tend = own_tend if layer < HALF else other_tend
        state[pl.ds(layer, SPEC, stride=LAYERS), :] = (
            moved[:SPEC] + tend[pl.ds(layer % HALF * SPAD, SPEC), :]
        )


def owner_result(own, other, state):
    order = place_of(lax.broadcasted_iota(jnp.int32, (COLS, COLS), 1))
    for block, begin in ((own, HALF), (other, 0)):
        for layer in range(HALF):
            for half in range(2):
                count = min(COLS, SPEC - half * COLS)
                turned = jnp.transpose(block[pl.ds(2 * layer + half, COLS, stride=LAYERS), :])
                turned = jnp.take_along_axis(turned, order, axis=1)
                state[pl.ds(half * COLS * LAYERS + begin + layer, count, stride=LAYERS), :] = (
                    turned[:count]
                )


def final_kernel(
    tile_of, tracers, wind, from_low, from_high, own_tend, other_tend, own, other, state
):
    @pl.when(tile_of[0] == 0)
    def _():
        advect(tile_of[1], tracers, wind, from_low, from_high, own_tend, other_tend, state)

    @pl.when(tile_of[0] == 1)
    def _():
        owner_result(own, other, state)


def cost(microseconds):
    return pl.CostEstimate(
        flops=int(microseconds * 1e9), bytes_accessed=int(microseconds * 2e6), transcendentals=0
    )


def bf16(*shape):
    return jax.ShapeDtypeStruct(shape, jnp.bfloat16)


def f32(*shape):
    return jax.ShapeDtypeStruct(shape, jnp.float32)


def local(
    species_amounts,
    air_warmth_kelvin,
    sunlight_strength,
    wind_stability_numbers,
    illuminated_marker,
    position_vertical_lookup,
    speed_constants,
    barrier_kelvins,
    consumed_species,
    outcome_species,
    outcome_fractions,
):
    tile_of = jnp.stack([lax.axis_index("group"), lax.axis_index("tile")]).astype(jnp.int32)
    amounts = species_amounts.reshape(ROWS, COLS)
    swap = [(0, 1), (1, 0)]
    swapped = lax.ppermute(amounts, "group", swap)

    weights, gather, terms = pl.pallas_call(
        prepare_kernel,
        out_shape=(
            bf16(3 * SPAD, RPAD),
            bf16(RPAD, KDIM),
            bf16(2 * (KDIM - SPAD), CELLS),
        ),
        in_specs=[SMEM] + [HBM] * 7,
        out_specs=(VMEM, VMEM, VMEM),
        scratch_shapes=[
            pltpu.VMEM((LAYERS, COLS), jnp.float32),
            pltpu.VMEM((LAYERS, COLS), jnp.float32),
            pltpu.VMEM((2, REAC), jnp.int32),
            pltpu.VMEM((2, REAC), jnp.int32),
            pltpu.VMEM((2, REAC), jnp.float32),
            pltpu.VMEM((1, REAC), jnp.float32),
            pltpu.VMEM((1, REAC), jnp.float32),
            pltpu.VMEM((KDIM, RPAD), jnp.float32),
            pltpu.SemaphoreType.DMA((7,)),
        ],
        compiler_params=PARAMS,
        cost_estimate=cost(1),
        name="prepare",
    )(
        tile_of,
        air_warmth_kelvin,
        sunlight_strength,
        consumed_species,
        outcome_species,
        outcome_fractions,
        speed_constants.reshape(1, REAC),
        barrier_kelvins.reshape(1, REAC),
    )
    send, tendency = pl.pallas_call(
        chemistry_kernel,
        out_shape=(f32(COLS * LAYERS, COLS), f32(HALF * SPAD, COLS)),
        in_specs=[SMEM, ANY, ANY] + [VMEM] * 5,
        out_specs=(VMEM, VMEM),
        scratch_shapes=[
            pltpu.VMEM((SPAD * LAYERS, COLS), jnp.float32),
            pltpu.VMEM((2 * KDIM, CELLS), jnp.bfloat16),
            pltpu.VMEM((SPAD, CELLS), jnp.float32),
            pltpu.VMEM((SPAD, CELLS), jnp.float32),
            pltpu.SemaphoreType.DMA(()),
        ],
        compiler_params=PARAMS,
        cost_estimate=cost(6),
        name="chemistry",
    )(
        tile_of,
        amounts,
        swapped,
        illuminated_marker.reshape(COLS, COLS),
        position_vertical_lookup.reshape(COLS, COLS),
        weights,
        gather,
        terms,
    )
    received = lax.all_to_all(
        send.reshape(COLS, LAYERS, COLS),
        "tile",
        split_axis=0,
        concat_axis=0,
        axis_index_groups=[ORDER],
        tiled=True,
    )

    edges = pl.pallas_call(
        edge_kernel,
        out_shape=f32(2 * EDGE * LAYERS, KDIM),
        in_specs=[VMEM, VMEM],
        out_specs=VMEM,
        scratch_shapes=[pltpu.VMEM((LAYERS, KDIM, COLS), jnp.float32)],
        compiler_params=PARAMS,
        cost_estimate=cost(1),
        name="edges",
    )(amounts, wind_stability_numbers)
    count = lax.axis_size("tile")
    from_low = lax.ppermute(edges, "tile", [(i, (i + 1) % count) for i in range(count)])
    from_high = lax.ppermute(edges, "tile", [((i + 1) % count, i) for i in range(count)])
    other_tendency = lax.ppermute(tendency, "group", swap)
    received, from_low, from_high, other_tendency = lax.optimization_barrier(
        (received, from_low, from_high, other_tendency)
    )
    received = received.reshape(COLS * LAYERS, COLS)
    other_received = lax.ppermute(received, "group", swap)
    state = pl.pallas_call(
        final_kernel,
        out_shape=f32(ROWS, COLS),
        in_specs=[SMEM] + [VMEM] * 8,
        out_specs=VMEM,
        compiler_params=PARAMS,
        cost_estimate=cost(2),
        name="final",
    )(
        tile_of,
        amounts,
        wind_stability_numbers,
        from_low,
        from_high,
        tendency,
        other_tendency,
        received,
        other_received,
    )
    return state.reshape(1, SPEC, LAYERS, COLS)


def solution(mesh):
    return jax.shard_map(
        local,
        mesh=mesh,
        in_specs=(
            P("group", None, None, "tile"),
            P(None, "tile"),
            P(None, "tile"),
            P(None, "tile"),
            P(),
            P(),
            P(),
            P(),
            P(),
            P(),
            P(),
        ),
        out_specs=P("group", None, None, "tile"),
        check_vma=False,
    )
```

```python
import jax
import jax.numpy as jnp
from jax import lax
from jax.experimental import pallas as pl
from jax.experimental.pallas import tpu as pltpu
from jax.sharding import PartitionSpec as P

SPEC = 220
REAC = 500
PHOT = 64
LAYERS = 8
COLS = 128
ADV_STEPS = 4
ITER_NIGHT = 2
ITER_DAY = 4

HALF = LAYERS // 2
ROWS = SPEC * LAYERS
SPAD = 224
KDIM = 256
RPAD = 512
CELLS = HALF * COLS
PIECES = 7
PACKED = PIECES * COLS
CHUNK = 256
EDGE = 4
DARK = -1024.0

MIDDLE = (4, 5, 3, 6, 2, 7, 1, 0)
ORDER = [z * 16 + x * 4 + y for y in range(3, -1, -1) for x in range(3, -1, -1) for z in MIDDLE]

VMEM = pl.BlockSpec(memory_space=pltpu.VMEM)
HBM = pl.BlockSpec(memory_space=pltpu.HBM)
PARAMS = pltpu.CompilerParams(vmem_limit_bytes=24 * 1024 * 1024)


def high_low(value):
    high = value.astype(jnp.bfloat16)
    return high, (value - high.astype(jnp.float32)).astype(jnp.bfloat16)


def dot(a, b):
    return jnp.dot(a, b, preferred_element_type=jnp.float32)


def tile_at(place):
    step = place % 8
    z = jnp.zeros_like(place)
    for at, value in enumerate(MIDDLE):
        z = jnp.where(step == at, value, z)
    return z * 16 + (3 - place // 8 % 4) * 4 + 3 - place // 32


def place_of(tile):
    z = tile // 16
    step = jnp.zeros_like(tile)
    for at, value in enumerate(MIDDLE):
        step = jnp.where(z == value, at, step)
    return (3 - tile % 4) * 32 + (3 - tile // 4 % 4) * 8 + step


def prepare_kernel(table, weights, gather, turning):
    spare = pl.ds(RPAD - COLS, COLS)
    weights[:, spare] = jnp.zeros((3 * SPAD, COLS), jnp.bfloat16)
    turning[:, spare] = jnp.zeros((KDIM, COLS), jnp.float32)
    row_of = [table[row : row + 1, :] for row in range(8)]

    used = pl.ds(0, REAC)
    species = lax.broadcasted_iota(jnp.int32, (SPAD, REAC), 0).astype(jnp.float32)
    thermal = lax.broadcasted_iota(jnp.int32, (1, REAC), 1) >= PHOT
    second = jnp.where(thermal, row_of[1], -1.0)
    consuming = jnp.where(species == row_of[0], 1.0, 0.0) + jnp.where(
        species == second, 1.0, 0.0
    )
    producing = jnp.where(species == row_of[2], row_of[4], 0.0) + jnp.where(
        species == row_of[3], row_of[5], 0.0
    )
    producing_high, producing_low = high_low(producing)
    weights[pl.ds(0, SPAD), used] = consuming.astype(jnp.bfloat16)
    weights[pl.ds(SPAD, SPAD), used] = producing_high
    weights[pl.ds(2 * SPAD, SPAD), used] = producing_low

    speed = lax.log2(row_of[6])
    speed_high = speed.astype(jnp.bfloat16).astype(jnp.float32)
    speed_mid = (speed - speed_high).astype(jnp.bfloat16).astype(jnp.float32)
    speed_low = speed - speed_high - speed_mid
    barrier = jnp.where(thermal, row_of[7], 0.0)
    barrier_high = barrier.astype(jnp.bfloat16).astype(jnp.float32)
    barrier_low = barrier - barrier_high
    photo = jnp.where(thermal, 0.0, 1.0)
    row = lax.broadcasted_iota(jnp.int32, (KDIM - SPAD, REAC), 0)
    extra = jnp.zeros((KDIM - SPAD, REAC), jnp.float32)
    for place, value in enumerate(
        (barrier_high, barrier_low, speed_high, speed_mid, speed_low, photo)
    ):
        extra = jnp.where(row == place, value, extra)
    turning[pl.ds(0, SPAD), used] = consuming
    turning[pl.ds(SPAD, KDIM - SPAD), used] = extra
    gather[...] = jnp.transpose(turning[...]).astype(jnp.bfloat16)


def chemistry_kernel(
    own,
    swapped,
    marker,
    lookup,
    heat,
    light,
    weights,
    gather,
    send,
    tendency,
    logs,
    start,
    now,
    stack,
    parts,
    packed,
    sems,
):
    group, tile = lax.axis_index("group"), lax.axis_index("tile")

    lit = jnp.max(marker[pl.ds(tile, 1), :])
    sweeps = jnp.where(lit > 0, ITER_DAY, ITER_NIGHT)
    row = lax.broadcasted_iota(jnp.int32, (KDIM - SPAD, COLS), 0)
    for layer in range(HALF):
        warmth = heat[pl.ds(group * HALF + layer, 1), :]
        flux = light[pl.ds(group * HALF + layer, 1), :]
        inverse = (1.0 / 250.0 - 1.0 / warmth) * 1.4426950408889634
        flux = jnp.where(lit > 0, lax.log2(flux), DARK)
        term = jnp.where(row < 2, inverse, 0.0)
        term = jnp.where((row >= 2) & (row < 5), 1.0, term)
        term = jnp.where(row == 5, flux, term)
        term_high, term_low = high_low(term)
        logs[SPAD:KDIM, pl.ds(layer * COLS, COLS)] = term_high
        logs[KDIM + SPAD :, pl.ds(layer * COLS, COLS)] = term_low
    for core, amounts in enumerate((swapped, own)):

        @pl.when(group == core)
        def _():
            for layer in range(HALF):
                begin = amounts[pl.ds(core * HALF + layer, SPEC, stride=LAYERS), :]
                start[0:SPEC, pl.ds(layer * COLS, COLS)] = begin

    start[SPEC:SPAD, :] = jnp.ones((SPAD - SPEC, CELLS), jnp.float32)
    now[...] = start[...]
    chunks = [pl.ds(at, CHUNK) for at in range(0, CELLS, CHUNK)]

    @pl.loop(0, sweeps)
    def _(_):
        for cells in chunks:
            log_high, log_low = high_low(lax.log2(now[:, cells]))
            logs[0:SPAD, cells] = log_high
            logs[KDIM : KDIM + SPAD, cells] = log_low
        for cells in chunks:
            rate = jnp.exp2(
                dot(gather[...], logs[0:KDIM, cells]) + dot(gather[...], logs[KDIM:, cells])
            )
            high, low = high_low(rate)
            both = dot(weights[0 : 2 * SPAD], high) + dot(weights[0 : 2 * SPAD], low)
            gain = both[SPAD:] + dot(weights[2 * SPAD :], high)
            concen = now[:, cells]
            now[:, cells] = concen * (start[:, cells] + gain) / (concen + both[:SPAD])

    lane = lax.broadcasted_iota(jnp.int32, (COLS, COLS), 1)
    column = jnp.sum(jnp.where(lane == tile, lookup[...], 0), axis=1, keepdims=True)
    pick = jnp.where(lane == column - tile * COLS, 1.0, 0.0)
    ordered = jnp.where(lane == tile_at(lax.broadcasted_iota(jnp.int32, (COLS, COLS), 0)), 1.0, 0.0)
    choose = dot(ordered.astype(jnp.bfloat16), pick.astype(jnp.bfloat16)).astype(jnp.bfloat16)
    for layer in range(HALF):
        cells = pl.ds(layer * COLS, COLS)
        stack[pl.ds(layer, SPEC, stride=HALF), :] = now[0:SPEC, cells]
    stack[HALF * SPEC :, :] = jnp.zeros((PACKED - HALF * SPEC, COLS), jnp.float32)
    for piece in range(PIECES):
        rest = jnp.transpose(stack[pl.ds(piece * COLS, COLS), :])
        for part in range(3):
            rounded = rest.astype(jnp.bfloat16)
            rest = rest - rounded.astype(jnp.float32)
            parts[pl.ds(part * COLS, COLS), pl.ds(piece * COLS, COLS)] = rounded
    copies = []
    for half in range(2):
        owners = COLS // 2
        turned = dot(
            jnp.concatenate([choose[half * owners : (half + 1) * owners]] * 3, axis=1), parts[...]
        )
        for piece in range(PIECES):
            packed[pl.ds(half * owners * PIECES + piece, owners, stride=PIECES), :] = turned[
                :, piece * COLS : (piece + 1) * COLS
            ]
        rows = pl.ds(half * owners * PIECES, owners * PIECES)
        copies.append(pltpu.make_async_copy(packed.at[rows], send.at[rows], sems.at[half]))
        copies[half].start()
    for layer in range(HALF):
        cells = pl.ds(layer * COLS, COLS)
        tendency[pl.ds(layer * SPAD, SPAD), :] = now[:, cells] - start[:, cells]
    for copy in copies:
        copy.wait()


def across(a, b):
    return lax.dot_general(a, b, (((1,), (1,)), ((), ())), preferred_element_type=jnp.float32)


def edge_kernel(tracers, wind, to_low, to_high, padded):
    row = lax.broadcasted_iota(jnp.int32, (2 * EDGE, COLS), 0)
    column = lax.broadcasted_iota(jnp.int32, (2 * EDGE, COLS), 1)
    pick = jnp.where(column == (row + COLS - EDGE) % COLS, 1.0, 0.0).astype(jnp.bfloat16)
    for layer in range(LAYERS):
        padded[layer, SPEC - 4 :, :] = jnp.zeros((KDIM - SPEC + 4, COLS), jnp.float32)
        padded[layer, 0:SPEC, :] = tracers[pl.ds(layer, SPEC, stride=LAYERS), :]
        padded[layer, SPEC : SPEC + 1, :] = wind[layer : layer + 1, :]
    for layer in range(LAYERS):
        high, low = high_low(padded[layer])
        picked = across(pick, high) + across(pick, low)
        to_high[pl.ds(layer * EDGE, EDGE), :] = picked[:EDGE]
        to_low[pl.ds(layer * EDGE, EDGE), :] = picked[EDGE:]


def advect(tracers, wind, from_low, from_high, own_tend, other_tend, state, after):
    tile = lax.axis_index("tile")
    side = EDGE * LAYERS
    low_there = jnp.where(tile > 0, 1.0, 0.0)
    high_there = jnp.where(tile < COLS - 1, 1.0, 0.0)
    beside = jnp.concatenate(
        [
            from_low[...] * low_there,
            from_high[...] * high_there,
            jnp.zeros((COLS - 2 * side, KDIM), jnp.float32),
        ],
        axis=0,
    )
    beside = jnp.transpose(beside)
    wind_row = jnp.broadcast_to(beside[SPEC : SPEC + 1, :], (LAYERS, COLS))
    layer_of = lax.broadcasted_iota(jnp.int32, (LAYERS, COLS), 0)
    right_half = lax.broadcasted_iota(jnp.int32, (LAYERS, COLS), 1) >= COLS // 2
    wind_side = jnp.zeros((LAYERS, COLS), jnp.float32)
    for layer in range(LAYERS):
        low = pltpu.roll(wind_row, COLS - EDGE - EDGE * layer, 1)
        high = pltpu.roll(wind_row, COLS - side - EDGE * layer, 1)
        wind_side = jnp.where(layer_of == layer, jnp.where(right_half, low, high), wind_side)

    lane = lax.broadcasted_iota(jnp.int32, (LAYERS, COLS), 1)
    lowest, highest = lane == 0, lane == COLS - 1

    def left(pair):
        up = [pltpu.roll(v, 1, 1) for v in pair]
        return jnp.where(lowest, up[1], up[0]), jnp.where(lowest, up[0], up[1])

    def right(pair):
        down = [pltpu.roll(v, COLS - 1, 1) for v in pair]
        return jnp.where(highest, down[1], down[0]), jnp.where(highest, down[0], down[1])

    factors = [
        (0.5 * c * (1.0 + c), 1.0 - c * c, 0.5 * c * (c - 1.0)) for c in (wind[...], wind_side)
    ]
    one = jnp.ones((LAYERS, COLS), jnp.float32)
    band = {0: (one, one)}
    for _ in range(ADV_STEPS):
        lefts = {d: left(pair) for d, pair in band.items()}
        rights = {d: right(pair) for d, pair in band.items()}
        reach = max(band) + 1
        fresh = {}
        for d in range(-reach, reach + 1):
            total = [0.0, 0.0]
            for source, factor in ((lefts.get(d + 1), 0), (band.get(d), 1), (rights.get(d - 1), 2)):
                if source is not None:
                    total = [t + factors[i][factor] * source[i] for i, t in enumerate(total)]
            fresh[d] = tuple(total)
        band = fresh

    rows = lax.broadcasted_iota(jnp.int32, (KDIM, COLS), 0)
    extra = rows - COLS
    edge = extra % EDGE
    place = jnp.where(rows < COLS, rows, jnp.where(extra < side, edge - EDGE, edge + COLS))
    offset = place - lax.broadcasted_iota(jnp.int32, (KDIM, COLS), 1)
    beside_high, beside_low = high_low(beside[:SPAD])
    for layer in range(LAYERS):
        here = (rows < COLS) | (extra % side // EDGE == layer)
        matrix = jnp.zeros((KDIM, COLS), jnp.float32)
        for d, (weight, _) in band.items():
            matrix = jnp.where(offset == d, weight[layer : layer + 1, :], matrix)
        matrix_high, matrix_low = high_low(jnp.where(here, matrix, 0.0))
        main = jnp.concatenate(
            [
                tracers[pl.ds(layer, SPEC, stride=LAYERS), :],
                jnp.zeros((SPAD - SPEC, COLS), jnp.float32),
            ],
            axis=0,
        )
        main_high, main_low = high_low(main)
        high = jnp.concatenate([main_high, beside_high], axis=1)
        low = jnp.concatenate([main_low, beside_low], axis=1)
        moved = dot(high, matrix_high) + dot(low, matrix_high) + dot(high, matrix_low)
        tend = own_tend if layer < HALF else other_tend
        state[pl.ds(layer, SPEC, stride=LAYERS), :] = (
            moved[:SPEC] + tend[pl.ds(layer % HALF * SPAD, SPEC), :]
        )
        after(layer)


def unpack(block, stack, state, begin, after):
    order = place_of(lax.broadcasted_iota(jnp.int32, (COLS, COLS), 1))
    for piece in range(PIECES):
        turned = jnp.transpose(block[pl.ds(piece, COLS, stride=PIECES), :])
        stack[pl.ds(piece * COLS, COLS), :] = jnp.take_along_axis(turned, order, axis=1)
        first, count = slab(piece)
        for layer in range(HALF):
            state[pl.ds(first * LAYERS + begin + layer, count, stride=LAYERS), :] = stack[
                pl.ds(piece * COLS + layer, count, stride=HALF), :
            ]
        after(piece)


def slab(piece):
    first = piece * COLS // HALF
    return first, min(COLS // HALF, SPEC - first)


def to_state(source, state, sem, first, count, begin):
    species, layers = pl.ds(first, count), pl.ds(begin, HALF)
    return pltpu.make_async_copy(
        source.reshape(SPEC, LAYERS, COLS).at[species, layers, :],
        state.reshape(SPEC, LAYERS, COLS).at[species, layers, :],
        sem,
    )


def first_kernel(
    tracers,
    wind,
    from_low,
    from_high,
    own_tend,
    other_tend,
    own,
    state,
    here,
    stack,
    sems,
):
    @pl.when(lax.axis_index("group") == 0)
    def _():
        def copy(layer):
            part = layer // HALF
            return to_state(here, state, sems.at[part], 0, SPEC, part * HALF)

        def after(layer):
            if layer % HALF == HALF - 1:
                copy(layer).start()

        advect(tracers, wind, from_low, from_high, own_tend, other_tend, here, after)
        for layer in (0, HALF):
            copy(layer).wait()

    @pl.when(lax.axis_index("group") == 1)
    def _():
        copies = [
            to_state(here, state, sems.at[piece], *slab(piece), HALF) for piece in range(PIECES)
        ]
        unpack(own, stack, here, HALF, lambda piece: copies[piece].start())
        for copy in copies:
            copy.wait()


def last_kernel(base, other, state, here, stack, sems):
    @pl.when(lax.axis_index("group") == 1)
    def _():
        copies = [
            to_state(here, state, sems.at[piece], *slab(piece), 0) for piece in range(PIECES)
        ]
        unpack(other, stack, here, 0, lambda piece: copies[piece].start())
        for copy in copies:
            copy.wait()


def cost(microseconds):
    return pl.CostEstimate(
        flops=int(microseconds * 1e9), bytes_accessed=int(microseconds * 2e6), transcendentals=0
    )


def bf16(*shape):
    return jax.ShapeDtypeStruct(shape, jnp.bfloat16)


def f32(*shape):
    return jax.ShapeDtypeStruct(shape, jnp.float32)


def local(
    species_amounts,
    air_warmth_kelvin,
    sunlight_strength,
    wind_stability_numbers,
    illuminated_marker,
    position_vertical_lookup,
    speed_constants,
    barrier_kelvins,
    consumed_species,
    outcome_species,
    outcome_fractions,
):
    amounts = species_amounts.reshape(ROWS, COLS)
    swap = [(0, 1), (1, 0)]
    swapped = lax.ppermute(amounts, "group", swap)

    table = jnp.concatenate(
        [
            consumed_species.astype(jnp.float32),
            outcome_species.astype(jnp.float32),
            outcome_fractions,
            speed_constants[None],
            barrier_kelvins[None],
        ]
    )
    weights, gather = pl.pallas_call(
        prepare_kernel,
        out_shape=(bf16(3 * SPAD, RPAD), bf16(RPAD, KDIM)),
        in_specs=[VMEM],
        out_specs=(VMEM, VMEM),
        scratch_shapes=[pltpu.VMEM((KDIM, RPAD), jnp.float32)],
        compiler_params=PARAMS,
        cost_estimate=cost(1),
        name="prepare",
    )(table)
    send, tendency = pl.pallas_call(
        chemistry_kernel,
        out_shape=(f32(PACKED, COLS), f32(HALF * SPAD, COLS)),
        in_specs=[VMEM] * 8,
        out_specs=(HBM, VMEM),
        scratch_shapes=[
            pltpu.VMEM((2 * KDIM, CELLS), jnp.bfloat16),
            pltpu.VMEM((SPAD, CELLS), jnp.float32),
            pltpu.VMEM((SPAD, CELLS), jnp.float32),
            pltpu.VMEM((PACKED, COLS), jnp.float32),
            pltpu.VMEM((3 * COLS, PACKED), jnp.bfloat16),
            pltpu.VMEM((PACKED, COLS), jnp.float32),
            pltpu.SemaphoreType.DMA((2,)),
        ],
        compiler_params=PARAMS,
        cost_estimate=cost(6),
        name="chemistry",
    )(
            amounts,
        swapped,
        illuminated_marker.reshape(COLS, COLS),
        position_vertical_lookup.reshape(COLS, COLS),
        air_warmth_kelvin,
        sunlight_strength,
        weights,
        gather,
    )
    received = lax.all_to_all(
        send.reshape(COLS, 1, PACKED),
        "tile",
        split_axis=0,
        concat_axis=0,
        axis_index_groups=[ORDER],
        tiled=True,
    )

    to_low, to_high = pl.pallas_call(
        edge_kernel,
        out_shape=(f32(EDGE * LAYERS, KDIM), f32(EDGE * LAYERS, KDIM)),
        in_specs=[VMEM, VMEM],
        out_specs=(VMEM, VMEM),
        scratch_shapes=[pltpu.VMEM((LAYERS, KDIM, COLS), jnp.float32)],
        compiler_params=PARAMS,
        cost_estimate=cost(1),
        name="edges",
    )(amounts, wind_stability_numbers)
    count = lax.axis_size("tile")
    both = ("group", "tile")
    from_low = lax.ppermute(to_high, both, [(i, i + 1) for i in range(count - 1)])
    from_high = lax.ppermute(to_low, both, [(i + 1, i) for i in range(count - 1)])
    other_tendency = lax.ppermute(tendency, "group", swap)
    received, other_tendency = lax.optimization_barrier((received, other_tendency))
    received = received.reshape(PACKED, COLS)
    other_received = lax.ppermute(received, "group", swap)
    base = pl.pallas_call(
        first_kernel,
        out_shape=f32(ROWS, COLS),
        in_specs=[VMEM] * 7,
        out_specs=HBM,
        scratch_shapes=[
            pltpu.VMEM((ROWS, COLS), jnp.float32),
            pltpu.VMEM((PACKED, COLS), jnp.float32),
            pltpu.SemaphoreType.DMA((PIECES,)),
        ],
        compiler_params=PARAMS,
        cost_estimate=cost(20),
        name="first",
    )(
            amounts,
        wind_stability_numbers,
        from_low,
        from_high,
        tendency,
        other_tendency,
        received,
    )
    state = pl.pallas_call(
        last_kernel,
        out_shape=f32(ROWS, COLS),
        in_specs=[HBM, VMEM],
        out_specs=HBM,
        input_output_aliases={0: 0},
        scratch_shapes=[
            pltpu.VMEM((ROWS, COLS), jnp.float32),
            pltpu.VMEM((PACKED, COLS), jnp.float32),
            pltpu.SemaphoreType.DMA((PIECES,)),
        ],
        compiler_params=PARAMS,
        cost_estimate=cost(1),
        name="last",
    )(base, other_received)
    return state.reshape(1, SPEC, LAYERS, COLS)


def solution(mesh):
    return jax.shard_map(
        local,
        mesh=mesh,
        in_specs=(
            P("group", None, None, "tile"),
            P(None, "tile"),
            P(None, "tile"),
            P(None, "tile"),
            P(),
            P(),
            P(),
            P(),
            P(),
            P(),
            P(),
        ),
        out_specs=P("group", None, None, "tile"),
        check_vma=False,
    )
```

```python
import jax
import jax.numpy as jnp
from jax import lax
from jax.experimental import pallas as pl
from jax.experimental.pallas import tpu as pltpu
from jax.sharding import PartitionSpec as P

SPEC = 220
REAC = 500
PHOT = 64
LAYERS = 8
COLS = 128
ADV_STEPS = 4
ITER_NIGHT = 2
ITER_DAY = 4

HALF = LAYERS // 2
ROWS = SPEC * LAYERS
SPAD = 224
KDIM = 256
RPAD = 512
CELLS = HALF * COLS
PIECES = 7
PACKED = PIECES * COLS
PARTS = 2
SENDS = 4
CHUNK = 256
EDGE = 4
DARK = -1024.0

MIDDLE = (4, 3, 5, 2, 6, 1, 7, 0)
INNER = (2, 1, 3, 0)
ORDER = [z * 16 + x * 4 + y for y in INNER for x in INNER for z in MIDDLE]

VMEM = pl.BlockSpec(memory_space=pltpu.VMEM)
HBM = pl.BlockSpec(memory_space=pltpu.HBM)
PARAMS = pltpu.CompilerParams(vmem_limit_bytes=24 * 1024 * 1024)


def high_low(value):
    high = value.astype(jnp.bfloat16)
    return high, (value - high.astype(jnp.float32)).astype(jnp.bfloat16)


def dot(a, b):
    return jnp.dot(a, b, preferred_element_type=jnp.float32)


def pick(table, index):
    out = jnp.zeros_like(index)
    for at, value in enumerate(table):
        out = jnp.where(index == at, value, out)
    return out


def tile_at(place):
    return pick(MIDDLE, place % 8) * 16 + pick(INNER, place // 8 % 4) * 4 + pick(INNER, place // 32)


def place_of(tile):
    middle = [MIDDLE.index(z) for z in range(8)]
    inner = [INNER.index(z) for z in range(4)]
    return pick(inner, tile % 4) * 32 + pick(inner, tile // 4 % 4) * 8 + pick(middle, tile // 16)


def prepare_kernel(table, weights, gather, turning):
    spare = pl.ds(RPAD - COLS, COLS)
    weights[:, spare] = jnp.zeros((3 * SPAD, COLS), jnp.bfloat16)
    turning[:, spare] = jnp.zeros((KDIM, COLS), jnp.float32)
    row_of = [table[row : row + 1, :] for row in range(8)]

    used = pl.ds(0, REAC)
    species = lax.broadcasted_iota(jnp.int32, (SPAD, REAC), 0).astype(jnp.float32)
    thermal = lax.broadcasted_iota(jnp.int32, (1, REAC), 1) >= PHOT
    second = jnp.where(thermal, row_of[1], -1.0)
    consuming = jnp.where(species == row_of[0], 1.0, 0.0) + jnp.where(
        species == second, 1.0, 0.0
    )
    producing = jnp.where(species == row_of[2], row_of[4], 0.0) + jnp.where(
        species == row_of[3], row_of[5], 0.0
    )
    producing_high, producing_low = high_low(producing)
    weights[pl.ds(0, SPAD), used] = consuming.astype(jnp.bfloat16)
    weights[pl.ds(SPAD, SPAD), used] = producing_high
    weights[pl.ds(2 * SPAD, SPAD), used] = producing_low

    speed = lax.log2(row_of[6])
    speed_high = speed.astype(jnp.bfloat16).astype(jnp.float32)
    speed_mid = (speed - speed_high).astype(jnp.bfloat16).astype(jnp.float32)
    speed_low = speed - speed_high - speed_mid
    barrier = jnp.where(thermal, row_of[7], 0.0)
    barrier_high = barrier.astype(jnp.bfloat16).astype(jnp.float32)
    barrier_low = barrier - barrier_high
    photo = jnp.where(thermal, 0.0, 1.0)
    row = lax.broadcasted_iota(jnp.int32, (KDIM - SPAD, REAC), 0)
    extra = jnp.zeros((KDIM - SPAD, REAC), jnp.float32)
    for place, value in enumerate(
        (barrier_high, barrier_low, speed_high, speed_mid, speed_low, photo)
    ):
        extra = jnp.where(row == place, value, extra)
    turning[pl.ds(0, SPAD), used] = consuming
    turning[pl.ds(SPAD, KDIM - SPAD), used] = extra
    gather[...] = jnp.transpose(turning[...]).astype(jnp.bfloat16)


def chemistry_kernel(
    own,
    swapped,
    marker,
    lookup,
    heat,
    light,
    weights,
    gather,
    send,
    tendency,
    logs,
    start,
    now,
    stack,
    parts,
    packed,
    sems,
):
    group, tile = lax.axis_index("group"), lax.axis_index("tile")

    lit = jnp.max(marker[pl.ds(tile, 1), :])
    sweeps = jnp.where(lit > 0, ITER_DAY, ITER_NIGHT)
    row = lax.broadcasted_iota(jnp.int32, (KDIM - SPAD, COLS), 0)
    for layer in range(HALF):
        warmth = heat[pl.ds(group * HALF + layer, 1), :]
        flux = light[pl.ds(group * HALF + layer, 1), :]
        inverse = (1.0 / 250.0 - 1.0 / warmth) * 1.4426950408889634
        flux = jnp.where(lit > 0, lax.log2(flux), DARK)
        term = jnp.where(row < 2, inverse, 0.0)
        term = jnp.where((row >= 2) & (row < 5), 1.0, term)
        term = jnp.where(row == 5, flux, term)
        term_high, term_low = high_low(term)
        logs[SPAD:KDIM, pl.ds(layer * COLS, COLS)] = term_high
        logs[KDIM + SPAD :, pl.ds(layer * COLS, COLS)] = term_low
    for core, amounts in enumerate((swapped, own)):

        @pl.when(group == core)
        def _():
            for layer in range(HALF):
                begin = amounts[pl.ds(core * HALF + layer, SPEC, stride=LAYERS), :]
                start[0:SPEC, pl.ds(layer * COLS, COLS)] = begin

    start[SPEC:SPAD, :] = jnp.ones((SPAD - SPEC, CELLS), jnp.float32)
    now[...] = start[...]
    chunks = [pl.ds(at, CHUNK) for at in range(0, CELLS, CHUNK)]

    def sweep():
        for cells in chunks:
            log_high, log_low = high_low(lax.log2(now[:, cells]))
            logs[0:SPAD, cells] = log_high
            logs[KDIM : KDIM + SPAD, cells] = log_low
        for cells in chunks:
            rate = jnp.exp2(
                dot(gather[...], logs[0:KDIM, cells]) + dot(gather[...], logs[KDIM:, cells])
            )
            high, low = high_low(rate)
            both = dot(weights[0 : 2 * SPAD], high) + dot(weights[0 : 2 * SPAD], low)
            gain = both[SPAD:] + dot(weights[2 * SPAD :], high)
            concen = now[:, cells]
            now[:, cells] = concen * (start[:, cells] + gain) / (concen + both[:SPAD])

    @pl.loop(0, sweeps // 2)
    def _(_):
        sweep()
        sweep()

    lane = lax.broadcasted_iota(jnp.int32, (COLS, COLS), 1)
    column = jnp.sum(jnp.where(lane == tile, lookup[...], 0), axis=1, keepdims=True)
    chosen = jnp.where(lane == column - tile * COLS, 1.0, 0.0)
    ordered = jnp.where(lane == tile_at(lax.broadcasted_iota(jnp.int32, (COLS, COLS), 0)), 1.0, 0.0)
    choose = dot(ordered.astype(jnp.bfloat16), chosen.astype(jnp.bfloat16)).astype(jnp.bfloat16)
    for layer in range(HALF):
        cells = pl.ds(layer * COLS, COLS)
        stack[pl.ds(layer, SPEC, stride=HALF), :] = now[0:SPEC, cells]
    stack[HALF * SPEC :, :] = jnp.zeros((PACKED - HALF * SPEC, COLS), jnp.float32)
    for piece in range(PIECES):
        rest = jnp.transpose(stack[pl.ds(piece * COLS, COLS), :])
        for part in range(PARTS):
            rounded = rest.astype(jnp.bfloat16)
            rest = rest - rounded.astype(jnp.float32)
            parts[pl.ds(part * COLS, COLS), pl.ds(piece * COLS, COLS)] = rounded
    copies = []
    owners = COLS // SENDS
    for part in range(SENDS):
        turned = dot(
            jnp.concatenate([choose[part * owners : (part + 1) * owners]] * PARTS, axis=1),
            parts[...],
        )
        for piece in range(PIECES):
            packed[pl.ds(part * owners * PIECES + piece, owners, stride=PIECES), :] = turned[
                :, piece * COLS : (piece + 1) * COLS
            ]
        rows = pl.ds(part * owners * PIECES, owners * PIECES)
        copies.append(pltpu.make_async_copy(packed.at[rows], send.at[rows], sems.at[part]))
        copies[part].start()
    for layer in range(HALF):
        cells = pl.ds(layer * COLS, COLS)
        tendency[pl.ds(layer * SPAD, SPAD), :] = now[:, cells] - start[:, cells]
    for copy in copies:
        copy.wait()


def across(a, b):
    return lax.dot_general(a, b, (((1,), (1,)), ((), ())), preferred_element_type=jnp.float32)


def edge_kernel(tracers, wind, far, near, padded):
    odd = lax.axis_index("tile") % 2 == 1
    row = lax.broadcasted_iota(jnp.int32, (2 * EDGE, COLS), 0)
    column = lax.broadcasted_iota(jnp.int32, (2 * EDGE, COLS), 1)
    choose = jnp.where(column == (row + COLS - EDGE) % COLS, 1.0, 0.0).astype(jnp.bfloat16)
    for layer in range(LAYERS):
        padded[layer, SPEC - 4 :, :] = jnp.zeros((KDIM - SPEC + 4, COLS), jnp.float32)
        padded[layer, 0:SPEC, :] = tracers[pl.ds(layer, SPEC, stride=LAYERS), :]
        padded[layer, SPEC : SPEC + 1, :] = wind[layer : layer + 1, :]
    for layer in range(LAYERS):
        high, low = high_low(padded[layer])
        picked = across(choose, high) + across(choose, low)
        to_high, to_low = picked[:EDGE], picked[EDGE:]
        far[pl.ds(layer * EDGE, EDGE), :] = jnp.where(odd, to_high, to_low)
        near[pl.ds(layer * EDGE, EDGE), :] = jnp.where(odd, to_low, to_high)


def advect(tracers, wind, far, near, own_tend, other_tend, state, after):
    tile = lax.axis_index("tile")
    odd = tile % 2 == 1
    side = EDGE * LAYERS
    low_there = jnp.where(tile > 0, 1.0, 0.0)
    high_there = jnp.where(tile < COLS - 1, 1.0, 0.0)
    beside = jnp.concatenate(
        [
            jnp.where(odd, near[...], far[...]) * low_there,
            jnp.where(odd, far[...], near[...]) * high_there,
            jnp.zeros((COLS - 2 * side, KDIM), jnp.float32),
        ],
        axis=0,
    )
    beside = jnp.transpose(beside)
    wind_row = jnp.broadcast_to(beside[SPEC : SPEC + 1, :], (LAYERS, COLS))
    layer_of = lax.broadcasted_iota(jnp.int32, (LAYERS, COLS), 0)
    right_half = lax.broadcasted_iota(jnp.int32, (LAYERS, COLS), 1) >= COLS // 2
    wind_side = jnp.zeros((LAYERS, COLS), jnp.float32)
    for layer in range(LAYERS):
        low = pltpu.roll(wind_row, COLS - EDGE - EDGE * layer, 1)
        high = pltpu.roll(wind_row, COLS - side - EDGE * layer, 1)
        wind_side = jnp.where(layer_of == layer, jnp.where(right_half, low, high), wind_side)

    lane = lax.broadcasted_iota(jnp.int32, (LAYERS, COLS), 1)
    lowest, highest = lane == 0, lane == COLS - 1

    def left(pair):
        up = [pltpu.roll(v, 1, 1) for v in pair]
        return jnp.where(lowest, up[1], up[0]), jnp.where(lowest, up[0], up[1])

    def right(pair):
        down = [pltpu.roll(v, COLS - 1, 1) for v in pair]
        return jnp.where(highest, down[1], down[0]), jnp.where(highest, down[0], down[1])

    factors = [
        (0.5 * c * (1.0 + c), 1.0 - c * c, 0.5 * c * (c - 1.0)) for c in (wind[...], wind_side)
    ]
    one = jnp.ones((LAYERS, COLS), jnp.float32)
    band = {0: (one, one)}
    for _ in range(ADV_STEPS):
        lefts = {d: left(pair) for d, pair in band.items()}
        rights = {d: right(pair) for d, pair in band.items()}
        reach = max(band) + 1
        fresh = {}
        for d in range(-reach, reach + 1):
            total = [0.0, 0.0]
            for source, factor in ((lefts.get(d + 1), 0), (band.get(d), 1), (rights.get(d - 1), 2)):
                if source is not None:
                    total = [t + factors[i][factor] * source[i] for i, t in enumerate(total)]
            fresh[d] = tuple(total)
        band = fresh

    rows = lax.broadcasted_iota(jnp.int32, (KDIM, COLS), 0)
    extra = rows - COLS
    edge = extra % EDGE
    place = jnp.where(rows < COLS, rows, jnp.where(extra < side, edge - EDGE, edge + COLS))
    offset = place - lax.broadcasted_iota(jnp.int32, (KDIM, COLS), 1)
    beside_high, beside_low = high_low(beside[:SPAD])
    for layer in range(LAYERS):
        here = (rows < COLS) | (extra % side // EDGE == layer)
        matrix = jnp.zeros((KDIM, COLS), jnp.float32)
        for d, (weight, _) in band.items():
            matrix = jnp.where(offset == d, weight[layer : layer + 1, :], matrix)
        matrix_high, matrix_low = high_low(jnp.where(here, matrix, 0.0))
        main = jnp.concatenate(
            [
                tracers[pl.ds(layer, SPEC, stride=LAYERS), :],
                jnp.zeros((SPAD - SPEC, COLS), jnp.float32),
            ],
            axis=0,
        )
        main_high, main_low = high_low(main)
        high = jnp.concatenate([main_high, beside_high], axis=1)
        low = jnp.concatenate([main_low, beside_low], axis=1)
        moved = dot(high, matrix_high) + dot(low, matrix_high) + dot(high, matrix_low)
        tend = own_tend if layer < HALF else other_tend
        state[pl.ds(layer, SPEC, stride=LAYERS), :] = (
            moved[:SPEC] + tend[pl.ds(layer % HALF * SPAD, SPEC), :]
        )
        after(layer)


def unpack(block, stack, state, begin, after):
    order = place_of(lax.broadcasted_iota(jnp.int32, (COLS, COLS), 1))
    for piece in range(PIECES):
        turned = jnp.transpose(block[pl.ds(piece, COLS, stride=PIECES), :])
        stack[pl.ds(piece * COLS, COLS), :] = jnp.take_along_axis(turned, order, axis=1)
        first, count = slab(piece)
        for layer in range(HALF):
            state[pl.ds(first * LAYERS + begin + layer, count, stride=LAYERS), :] = stack[
                pl.ds(piece * COLS + layer, count, stride=HALF), :
            ]
        after(piece)


def slab(piece):
    first = piece * COLS // HALF
    return first, min(COLS // HALF, SPEC - first)


def to_state(source, state, sem, first, count, begin):
    species, layers = pl.ds(first, count), pl.ds(begin, HALF)
    return pltpu.make_async_copy(
        source.reshape(SPEC, LAYERS, COLS).at[species, layers, :],
        state.reshape(SPEC, LAYERS, COLS).at[species, layers, :],
        sem,
    )


def first_kernel(
    tracers,
    wind,
    far,
    near,
    own_tend,
    other_tend,
    own,
    state,
    here,
    stack,
    sems,
):
    @pl.when(lax.axis_index("group") == 0)
    def _():
        def copy(layer):
            part = layer // HALF
            return to_state(here, state, sems.at[part], 0, SPEC, part * HALF)

        def after(layer):
            if layer % HALF == HALF - 1:
                copy(layer).start()

        advect(tracers, wind, far, near, own_tend, other_tend, here, after)
        for layer in (0, HALF):
            copy(layer).wait()

    @pl.when(lax.axis_index("group") == 1)
    def _():
        copies = [
            to_state(here, state, sems.at[piece], *slab(piece), HALF) for piece in range(PIECES)
        ]
        unpack(own, stack, here, HALF, lambda piece: copies[piece].start())
        for copy in copies:
            copy.wait()


def last_kernel(base, other, state, here, stack, sems):
    @pl.when(lax.axis_index("group") == 1)
    def _():
        copies = [
            to_state(here, state, sems.at[piece], *slab(piece), 0) for piece in range(PIECES)
        ]
        unpack(other, stack, here, 0, lambda piece: copies[piece].start())
        for copy in copies:
            copy.wait()


def cost(microseconds):
    return pl.CostEstimate(
        flops=int(microseconds * 1e9), bytes_accessed=int(microseconds * 2e6), transcendentals=0
    )


def bf16(*shape):
    return jax.ShapeDtypeStruct(shape, jnp.bfloat16)


def f32(*shape):
    return jax.ShapeDtypeStruct(shape, jnp.float32)


def exchanged(tiles):
    return [pair for i in tiles for pair in ((i, i + 1), (i + 1, i))]


def local(
    species_amounts,
    air_warmth_kelvin,
    sunlight_strength,
    wind_stability_numbers,
    illuminated_marker,
    position_vertical_lookup,
    speed_constants,
    barrier_kelvins,
    consumed_species,
    outcome_species,
    outcome_fractions,
):
    amounts = species_amounts.reshape(ROWS, COLS)
    swap = [(0, 1), (1, 0)]
    swapped = lax.ppermute(amounts, "group", swap)

    table = jnp.concatenate(
        [
            consumed_species.astype(jnp.float32),
            outcome_species.astype(jnp.float32),
            outcome_fractions,
            speed_constants[None],
            barrier_kelvins[None],
        ]
    )
    weights, gather = pl.pallas_call(
        prepare_kernel,
        out_shape=(bf16(3 * SPAD, RPAD), bf16(RPAD, KDIM)),
        in_specs=[VMEM],
        out_specs=(VMEM, VMEM),
        scratch_shapes=[pltpu.VMEM((KDIM, RPAD), jnp.float32)],
        compiler_params=PARAMS,
        cost_estimate=cost(1),
        name="prepare",
    )(table)
    send, tendency = pl.pallas_call(
        chemistry_kernel,
        out_shape=(f32(PACKED, COLS), f32(HALF * SPAD, COLS)),
        in_specs=[VMEM] * 8,
        out_specs=(HBM, VMEM),
        scratch_shapes=[
            pltpu.VMEM((2 * KDIM, CELLS), jnp.bfloat16),
            pltpu.VMEM((SPAD, CELLS), jnp.float32),
            pltpu.VMEM((SPAD, CELLS), jnp.float32),
            pltpu.VMEM((PACKED, COLS), jnp.float32),
            pltpu.VMEM((PARTS * COLS, PACKED), jnp.bfloat16),
            pltpu.VMEM((PACKED, COLS), jnp.float32),
            pltpu.SemaphoreType.DMA((SENDS,)),
        ],
        compiler_params=PARAMS,
        cost_estimate=cost(6),
        name="chemistry",
    )(
            amounts,
        swapped,
        illuminated_marker.reshape(COLS, COLS),
        position_vertical_lookup.reshape(COLS, COLS),
        air_warmth_kelvin,
        sunlight_strength,
        weights,
        gather,
    )
    received = lax.all_to_all(
        send.reshape(COLS, 1, PACKED),
        "tile",
        split_axis=0,
        concat_axis=0,
        axis_index_groups=[ORDER],
        tiled=True,
    )

    far, near = pl.pallas_call(
        edge_kernel,
        out_shape=(f32(EDGE * LAYERS, KDIM), f32(EDGE * LAYERS, KDIM)),
        in_specs=[VMEM, VMEM],
        out_specs=(VMEM, VMEM),
        scratch_shapes=[pltpu.VMEM((LAYERS, KDIM, COLS), jnp.float32)],
        compiler_params=PARAMS,
        cost_estimate=cost(1),
        name="edges",
    )(amounts, wind_stability_numbers)
    count = lax.axis_size("tile")
    both = ("group", "tile")
    far = lax.ppermute(far, both, exchanged(range(1, count - 1, 2)))
    near = lax.ppermute(near, both, exchanged(range(0, count, 2)))
    other_tendency = lax.ppermute(tendency, "group", swap)
    received, other_tendency = lax.optimization_barrier((received, other_tendency))
    received = received.reshape(PACKED, COLS)
    other_received = lax.ppermute(received, "group", swap)
    base = pl.pallas_call(
        first_kernel,
        out_shape=f32(ROWS, COLS),
        in_specs=[VMEM] * 7,
        out_specs=HBM,
        scratch_shapes=[
            pltpu.VMEM((ROWS, COLS), jnp.float32),
            pltpu.VMEM((PACKED, COLS), jnp.float32),
            pltpu.SemaphoreType.DMA((PIECES,)),
        ],
        compiler_params=PARAMS,
        cost_estimate=cost(20),
        name="first",
    )(
            amounts,
        wind_stability_numbers,
        far,
        near,
        tendency,
        other_tendency,
        received,
    )
    state = pl.pallas_call(
        last_kernel,
        out_shape=f32(ROWS, COLS),
        in_specs=[HBM, VMEM],
        out_specs=HBM,
        input_output_aliases={0: 0},
        scratch_shapes=[
            pltpu.VMEM((ROWS, COLS), jnp.float32),
            pltpu.VMEM((PACKED, COLS), jnp.float32),
            pltpu.SemaphoreType.DMA((PIECES,)),
        ],
        compiler_params=PARAMS,
        cost_estimate=cost(1),
        name="last",
    )(base, other_received)
    return state.reshape(1, SPEC, LAYERS, COLS)


def solution(mesh):
    return jax.shard_map(
        local,
        mesh=mesh,
        in_specs=(
            P("group", None, None, "tile"),
            P(None, "tile"),
            P(None, "tile"),
            P(None, "tile"),
            P(),
            P(),
            P(),
            P(),
            P(),
            P(),
            P(),
        ),
        out_specs=P("group", None, None, "tile"),
        check_vma=False,
    )
```

```python
import jax
import jax.numpy as jnp
from jax import lax
from jax.experimental import pallas as pl
from jax.experimental.pallas import tpu as pltpu
from jax.sharding import PartitionSpec as P

SPEC = 220
REAC = 500
PHOT = 64
LAYERS = 8
COLS = 128
ADV_STEPS = 4
ITER_NIGHT = 2
ITER_DAY = 4

HALF = LAYERS // 2
ROWS = SPEC * LAYERS
SPAD = 224
KDIM = 256
RPAD = 512
CELLS = HALF * COLS
PIECES = 7
PACKED = PIECES * COLS
PARTS = 2
SENDS = 1
CHUNK = 256
EDGE = 4
DARK = -1024.0

MIDDLE = (4, 3, 5, 2, 6, 1, 7, 0)
INNER = (2, 1, 3, 0)
ORDER = [z * 16 + x * 4 + y for z in MIDDLE for x in INNER for y in INNER]

VMEM = pl.BlockSpec(memory_space=pltpu.VMEM)
HBM = pl.BlockSpec(memory_space=pltpu.HBM)
PARAMS = pltpu.CompilerParams(vmem_limit_bytes=24 * 1024 * 1024)


def high_low(value):
    high = value.astype(jnp.bfloat16)
    return high, (value - high.astype(jnp.float32)).astype(jnp.bfloat16)


def dot(a, b):
    return jnp.dot(a, b, preferred_element_type=jnp.float32)


def pick(table, index):
    out = jnp.zeros_like(index)
    for at, value in enumerate(table):
        out = jnp.where(index == at, value, out)
    return out


def tile_at(place):
    return pick(MIDDLE, place // 16) * 16 + pick(INNER, place // 4 % 4) * 4 + pick(INNER, place % 4)


def place_of(tile):
    middle = [MIDDLE.index(z) for z in range(8)]
    inner = [INNER.index(z) for z in range(4)]
    return pick(middle, tile // 16) * 16 + pick(inner, tile // 4 % 4) * 4 + pick(inner, tile % 4)


def prepare_kernel(table, weights, gather, turning):
    spare = pl.ds(RPAD - COLS, COLS)
    weights[:, spare] = jnp.zeros((3 * SPAD, COLS), jnp.bfloat16)
    turning[:, spare] = jnp.zeros((KDIM, COLS), jnp.float32)
    row_of = [table[row : row + 1, :] for row in range(8)]

    used = pl.ds(0, REAC)
    species = lax.broadcasted_iota(jnp.int32, (SPAD, REAC), 0).astype(jnp.float32)
    thermal = lax.broadcasted_iota(jnp.int32, (1, REAC), 1) >= PHOT
    second = jnp.where(thermal, row_of[1], -1.0)
    consuming = jnp.where(species == row_of[0], 1.0, 0.0) + jnp.where(
        species == second, 1.0, 0.0
    )
    producing = jnp.where(species == row_of[2], row_of[4], 0.0) + jnp.where(
        species == row_of[3], row_of[5], 0.0
    )
    producing_high, producing_low = high_low(producing)
    weights[pl.ds(0, SPAD), used] = consuming.astype(jnp.bfloat16)
    weights[pl.ds(SPAD, SPAD), used] = producing_high
    weights[pl.ds(2 * SPAD, SPAD), used] = producing_low

    speed = lax.log2(row_of[6])
    speed_high = speed.astype(jnp.bfloat16).astype(jnp.float32)
    speed_mid = (speed - speed_high).astype(jnp.bfloat16).astype(jnp.float32)
    speed_low = speed - speed_high - speed_mid
    barrier = jnp.where(thermal, row_of[7], 0.0)
    barrier_high = barrier.astype(jnp.bfloat16).astype(jnp.float32)
    barrier_low = barrier - barrier_high
    photo = jnp.where(thermal, 0.0, 1.0)
    row = lax.broadcasted_iota(jnp.int32, (KDIM - SPAD, REAC), 0)
    extra = jnp.zeros((KDIM - SPAD, REAC), jnp.float32)
    for place, value in enumerate(
        (barrier_high, barrier_low, speed_high, speed_mid, speed_low, photo)
    ):
        extra = jnp.where(row == place, value, extra)
    turning[pl.ds(0, SPAD), used] = consuming
    turning[pl.ds(SPAD, KDIM - SPAD), used] = extra
    gather[...] = jnp.transpose(turning[...]).astype(jnp.bfloat16)


def chemistry_kernel(
    own,
    swapped,
    marker,
    lookup,
    heat,
    light,
    weights,
    gather,
    send,
    tendency,
    logs,
    start,
    now,
    stack,
    parts,
    packed,
    sems,
):
    group, tile = lax.axis_index("group"), lax.axis_index("tile")

    lit = jnp.max(marker[pl.ds(tile, 1), :])
    sweeps = jnp.where(lit > 0, ITER_DAY, ITER_NIGHT)
    row = lax.broadcasted_iota(jnp.int32, (KDIM - SPAD, COLS), 0)
    for layer in range(HALF):
        warmth = heat[pl.ds(group * HALF + layer, 1), :]
        flux = light[pl.ds(group * HALF + layer, 1), :]
        inverse = (1.0 / 250.0 - 1.0 / warmth) * 1.4426950408889634
        flux = jnp.where(lit > 0, lax.log2(flux), DARK)
        term = jnp.where(row < 2, inverse, 0.0)
        term = jnp.where((row >= 2) & (row < 5), 1.0, term)
        term = jnp.where(row == 5, flux, term)
        term_high, term_low = high_low(term)
        logs[SPAD:KDIM, pl.ds(layer * COLS, COLS)] = term_high
        logs[KDIM + SPAD :, pl.ds(layer * COLS, COLS)] = term_low
    for core, amounts in enumerate((swapped, own)):

        @pl.when(group == core)
        def _():
            for layer in range(HALF):
                begin = amounts[pl.ds(core * HALF + layer, SPEC, stride=LAYERS), :]
                start[0:SPEC, pl.ds(layer * COLS, COLS)] = begin

    start[SPEC:SPAD, :] = jnp.ones((SPAD - SPEC, CELLS), jnp.float32)
    now[...] = start[...]
    chunks = [pl.ds(at, CHUNK) for at in range(0, CELLS, CHUNK)]

    def sweep():
        for cells in chunks:
            log_high, log_low = high_low(lax.log2(now[:, cells]))
            logs[0:SPAD, cells] = log_high
            logs[KDIM : KDIM + SPAD, cells] = log_low
        for cells in chunks:
            rate = jnp.exp2(
                dot(gather[...], logs[0:KDIM, cells]) + dot(gather[...], logs[KDIM:, cells])
            )
            high, low = high_low(rate)
            both = dot(weights[0 : 2 * SPAD], high) + dot(weights[0 : 2 * SPAD], low)
            gain = both[SPAD:] + dot(weights[2 * SPAD :], high)
            concen = now[:, cells]
            now[:, cells] = concen * (start[:, cells] + gain) / (concen + both[:SPAD])

    @pl.loop(0, sweeps // 2)
    def _(_):
        sweep()
        sweep()

    lane = lax.broadcasted_iota(jnp.int32, (COLS, COLS), 1)
    column = jnp.sum(jnp.where(lane == tile, lookup[...], 0), axis=1, keepdims=True)
    chosen = jnp.where(lane == column - tile * COLS, 1.0, 0.0)
    ordered = jnp.where(lane == tile_at(lax.broadcasted_iota(jnp.int32, (COLS, COLS), 0)), 1.0, 0.0)
    choose = dot(ordered.astype(jnp.bfloat16), chosen.astype(jnp.bfloat16)).astype(jnp.bfloat16)
    for layer in range(HALF):
        cells = pl.ds(layer * COLS, COLS)
        stack[pl.ds(layer, SPEC, stride=HALF), :] = now[0:SPEC, cells]
    stack[HALF * SPEC :, :] = jnp.zeros((PACKED - HALF * SPEC, COLS), jnp.float32)
    for piece in range(PIECES):
        rest = jnp.transpose(stack[pl.ds(piece * COLS, COLS), :])
        for part in range(PARTS):
            rounded = rest.astype(jnp.bfloat16)
            rest = rest - rounded.astype(jnp.float32)
            parts[pl.ds(part * COLS, COLS), pl.ds(piece * COLS, COLS)] = rounded
    copies = []
    owners = COLS // SENDS
    for part in range(SENDS):
        turned = dot(
            jnp.concatenate([choose[part * owners : (part + 1) * owners]] * PARTS, axis=1),
            parts[...],
        )
        for piece in range(PIECES):
            packed[pl.ds(part * owners * PIECES + piece, owners, stride=PIECES), :] = turned[
                :, piece * COLS : (piece + 1) * COLS
            ]
        rows = pl.ds(part * owners * PIECES, owners * PIECES)
        copies.append(pltpu.make_async_copy(packed.at[rows], send.at[rows], sems.at[part]))
        copies[part].start()
    for layer in range(HALF):
        cells = pl.ds(layer * COLS, COLS)
        tendency[pl.ds(layer * SPAD, SPAD), :] = now[:, cells] - start[:, cells]
    for copy in copies:
        copy.wait()


def across(a, b):
    return lax.dot_general(a, b, (((1,), (1,)), ((), ())), preferred_element_type=jnp.float32)


def edge_kernel(tracers, wind, far, near, padded):
    odd = lax.axis_index("tile") % 2 == 1
    row = lax.broadcasted_iota(jnp.int32, (2 * EDGE, COLS), 0)
    column = lax.broadcasted_iota(jnp.int32, (2 * EDGE, COLS), 1)
    choose = jnp.where(column == (row + COLS - EDGE) % COLS, 1.0, 0.0).astype(jnp.bfloat16)
    for layer in range(LAYERS):
        padded[layer, SPEC - 4 :, :] = jnp.zeros((KDIM - SPEC + 4, COLS), jnp.float32)
        padded[layer, 0:SPEC, :] = tracers[pl.ds(layer, SPEC, stride=LAYERS), :]
        padded[layer, SPEC : SPEC + 1, :] = wind[layer : layer + 1, :]
    for layer in range(LAYERS):
        high, low = high_low(padded[layer])
        picked = across(choose, high) + across(choose, low)
        to_high, to_low = picked[:EDGE], picked[EDGE:]
        far[pl.ds(layer * EDGE, EDGE), :] = jnp.where(odd, to_high, to_low)
        near[pl.ds(layer * EDGE, EDGE), :] = jnp.where(odd, to_low, to_high)


def advect(tracers, wind, far, near, own_tend, other_tend, state, after):
    tile = lax.axis_index("tile")
    odd = tile % 2 == 1
    side = EDGE * LAYERS
    low_there = jnp.where(tile > 0, 1.0, 0.0)
    high_there = jnp.where(tile < COLS - 1, 1.0, 0.0)
    beside = jnp.concatenate(
        [
            jnp.where(odd, near[...], far[...]) * low_there,
            jnp.where(odd, far[...], near[...]) * high_there,
            jnp.zeros((COLS - 2 * side, KDIM), jnp.float32),
        ],
        axis=0,
    )
    beside = jnp.transpose(beside)
    wind_row = jnp.broadcast_to(beside[SPEC : SPEC + 1, :], (LAYERS, COLS))
    layer_of = lax.broadcasted_iota(jnp.int32, (LAYERS, COLS), 0)
    right_half = lax.broadcasted_iota(jnp.int32, (LAYERS, COLS), 1) >= COLS // 2
    wind_side = jnp.zeros((LAYERS, COLS), jnp.float32)
    for layer in range(LAYERS):
        low = pltpu.roll(wind_row, COLS - EDGE - EDGE * layer, 1)
        high = pltpu.roll(wind_row, COLS - side - EDGE * layer, 1)
        wind_side = jnp.where(layer_of == layer, jnp.where(right_half, low, high), wind_side)

    lane = lax.broadcasted_iota(jnp.int32, (LAYERS, COLS), 1)
    lowest, highest = lane == 0, lane == COLS - 1

    def left(pair):
        up = [pltpu.roll(v, 1, 1) for v in pair]
        return jnp.where(lowest, up[1], up[0]), jnp.where(lowest, up[0], up[1])

    def right(pair):
        down = [pltpu.roll(v, COLS - 1, 1) for v in pair]
        return jnp.where(highest, down[1], down[0]), jnp.where(highest, down[0], down[1])

    factors = [
        (0.5 * c * (1.0 + c), 1.0 - c * c, 0.5 * c * (c - 1.0)) for c in (wind[...], wind_side)
    ]
    one = jnp.ones((LAYERS, COLS), jnp.float32)
    band = {0: (one, one)}
    for _ in range(ADV_STEPS):
        lefts = {d: left(pair) for d, pair in band.items()}
        rights = {d: right(pair) for d, pair in band.items()}
        reach = max(band) + 1
        fresh = {}
        for d in range(-reach, reach + 1):
            total = [0.0, 0.0]
            for source, factor in ((lefts.get(d + 1), 0), (band.get(d), 1), (rights.get(d - 1), 2)):
                if source is not None:
                    total = [t + factors[i][factor] * source[i] for i, t in enumerate(total)]
            fresh[d] = tuple(total)
        band = fresh

    rows = lax.broadcasted_iota(jnp.int32, (KDIM, COLS), 0)
    extra = rows - COLS
    edge = extra % EDGE
    place = jnp.where(rows < COLS, rows, jnp.where(extra < side, edge - EDGE, edge + COLS))
    offset = place - lax.broadcasted_iota(jnp.int32, (KDIM, COLS), 1)
    beside_high, beside_low = high_low(beside[:SPAD])
    for layer in range(LAYERS):
        here = (rows < COLS) | (extra % side // EDGE == layer)
        matrix = jnp.zeros((KDIM, COLS), jnp.float32)
        for d, (weight, _) in band.items():
            matrix = jnp.where(offset == d, weight[layer : layer + 1, :], matrix)
        matrix_high, matrix_low = high_low(jnp.where(here, matrix, 0.0))
        main = jnp.concatenate(
            [
                tracers[pl.ds(layer, SPEC, stride=LAYERS), :],
                jnp.zeros((SPAD - SPEC, COLS), jnp.float32),
            ],
            axis=0,
        )
        main_high, main_low = high_low(main)
        high = jnp.concatenate([main_high, beside_high], axis=1)
        low = jnp.concatenate([main_low, beside_low], axis=1)
        moved = dot(high, matrix_high) + dot(low, matrix_high) + dot(high, matrix_low)
        tend = own_tend if layer < HALF else other_tend
        state[pl.ds(layer, SPEC, stride=LAYERS), :] = (
            moved[:SPEC] + tend[pl.ds(layer % HALF * SPAD, SPEC), :]
        )
        after(layer)


def unpack(block, stack, state, begin, after):
    order = place_of(lax.broadcasted_iota(jnp.int32, (COLS, COLS), 1))
    for piece in range(PIECES):
        turned = jnp.transpose(block[pl.ds(piece, COLS, stride=PIECES), :])
        stack[pl.ds(piece * COLS, COLS), :] = jnp.take_along_axis(turned, order, axis=1)
        first, count = slab(piece)
        for layer in range(HALF):
            state[pl.ds(first * LAYERS + begin + layer, count, stride=LAYERS), :] = stack[
                pl.ds(piece * COLS + layer, count, stride=HALF), :
            ]
        after(piece)


def slab(piece):
    first = piece * COLS // HALF
    return first, min(COLS // HALF, SPEC - first)


def to_state(source, state, sem, first, count, begin):
    species, layers = pl.ds(first, count), pl.ds(begin, HALF)
    return pltpu.make_async_copy(
        source.reshape(SPEC, LAYERS, COLS).at[species, layers, :],
        state.reshape(SPEC, LAYERS, COLS).at[species, layers, :],
        sem,
    )


def first_kernel(
    tracers,
    wind,
    far,
    near,
    own_tend,
    other_tend,
    own,
    state,
    here,
    stack,
    sems,
):
    @pl.when(lax.axis_index("group") == 0)
    def _():
        def copy(layer):
            part = layer // HALF
            return to_state(here, state, sems.at[part], 0, SPEC, part * HALF)

        def after(layer):
            if layer % HALF == HALF - 1:
                copy(layer).start()

        advect(tracers, wind, far, near, own_tend, other_tend, here, after)
        for layer in (0, HALF):
            copy(layer).wait()

    @pl.when(lax.axis_index("group") == 1)
    def _():
        copies = [
            to_state(here, state, sems.at[piece], *slab(piece), HALF) for piece in range(PIECES)
        ]
        unpack(own, stack, here, HALF, lambda piece: copies[piece].start())
        for copy in copies:
            copy.wait()


def last_kernel(base, other, state, here, stack, sems):
    @pl.when(lax.axis_index("group") == 1)
    def _():
        copies = [
            to_state(here, state, sems.at[piece], *slab(piece), 0) for piece in range(PIECES)
        ]
        unpack(other, stack, here, 0, lambda piece: copies[piece].start())
        for copy in copies:
            copy.wait()


def cost(microseconds):
    return pl.CostEstimate(
        flops=int(microseconds * 1e9), bytes_accessed=int(microseconds * 2e6), transcendentals=0
    )


def bf16(*shape):
    return jax.ShapeDtypeStruct(shape, jnp.bfloat16)


def f32(*shape):
    return jax.ShapeDtypeStruct(shape, jnp.float32)


def exchanged(tiles):
    return [pair for i in tiles for pair in ((i, i + 1), (i + 1, i))]


def local(
    species_amounts,
    air_warmth_kelvin,
    sunlight_strength,
    wind_stability_numbers,
    illuminated_marker,
    position_vertical_lookup,
    speed_constants,
    barrier_kelvins,
    consumed_species,
    outcome_species,
    outcome_fractions,
):
    amounts = species_amounts.reshape(ROWS, COLS)
    swap = [(0, 1), (1, 0)]
    swapped = lax.ppermute(amounts, "group", swap)

    table = jnp.concatenate(
        [
            consumed_species.astype(jnp.float32),
            outcome_species.astype(jnp.float32),
            outcome_fractions,
            speed_constants[None],
            barrier_kelvins[None],
        ]
    )
    weights, gather = pl.pallas_call(
        prepare_kernel,
        out_shape=(bf16(3 * SPAD, RPAD), bf16(RPAD, KDIM)),
        in_specs=[VMEM],
        out_specs=(VMEM, VMEM),
        scratch_shapes=[pltpu.VMEM((KDIM, RPAD), jnp.float32)],
        compiler_params=PARAMS,
        cost_estimate=cost(1),
        name="prepare",
    )(table)
    send, tendency = pl.pallas_call(
        chemistry_kernel,
        out_shape=(f32(PACKED, COLS), f32(HALF * SPAD, COLS)),
        in_specs=[VMEM] * 8,
        out_specs=(HBM, VMEM),
        scratch_shapes=[
            pltpu.VMEM((2 * KDIM, CELLS), jnp.bfloat16),
            pltpu.VMEM((SPAD, CELLS), jnp.float32),
            pltpu.VMEM((SPAD, CELLS), jnp.float32),
            pltpu.VMEM((PACKED, COLS), jnp.float32),
            pltpu.VMEM((PARTS * COLS, PACKED), jnp.bfloat16),
            pltpu.VMEM((PACKED, COLS), jnp.float32),
            pltpu.SemaphoreType.DMA((SENDS,)),
        ],
        compiler_params=PARAMS,
        cost_estimate=cost(6),
        name="chemistry",
    )(
            amounts,
        swapped,
        illuminated_marker.reshape(COLS, COLS),
        position_vertical_lookup.reshape(COLS, COLS),
        air_warmth_kelvin,
        sunlight_strength,
        weights,
        gather,
    )
    received = lax.all_to_all(
        send.reshape(COLS, 1, PACKED),
        "tile",
        split_axis=0,
        concat_axis=0,
        axis_index_groups=[ORDER],
        tiled=True,
    )

    far, near = pl.pallas_call(
        edge_kernel,
        out_shape=(f32(EDGE * LAYERS, KDIM), f32(EDGE * LAYERS, KDIM)),
        in_specs=[VMEM, VMEM],
        out_specs=(VMEM, VMEM),
        scratch_shapes=[pltpu.VMEM((LAYERS, KDIM, COLS), jnp.float32)],
        compiler_params=PARAMS,
        cost_estimate=cost(1),
        name="edges",
    )(amounts, wind_stability_numbers)
    count = lax.axis_size("tile")
    both = ("group", "tile")
    far = lax.ppermute(far, both, exchanged(range(1, count - 1, 2)))
    near = lax.ppermute(near, both, exchanged(range(0, count, 2)))
    other_tendency = lax.ppermute(tendency, "group", swap)
    received, other_tendency = lax.optimization_barrier((received, other_tendency))
    received = received.reshape(PACKED, COLS)
    other_received = lax.ppermute(received, "group", swap)
    base = pl.pallas_call(
        first_kernel,
        out_shape=f32(ROWS, COLS),
        in_specs=[VMEM] * 7,
        out_specs=HBM,
        scratch_shapes=[
            pltpu.VMEM((ROWS, COLS), jnp.float32),
            pltpu.VMEM((PACKED, COLS), jnp.float32),
            pltpu.SemaphoreType.DMA((PIECES,)),
        ],
        compiler_params=PARAMS,
        cost_estimate=cost(20),
        name="first",
    )(
            amounts,
        wind_stability_numbers,
        far,
        near,
        tendency,
        other_tendency,
        received,
    )
    state = pl.pallas_call(
        last_kernel,
        out_shape=f32(ROWS, COLS),
        in_specs=[HBM, VMEM],
        out_specs=HBM,
        input_output_aliases={0: 0},
        scratch_shapes=[
            pltpu.VMEM((ROWS, COLS), jnp.float32),
            pltpu.VMEM((PACKED, COLS), jnp.float32),
            pltpu.SemaphoreType.DMA((PIECES,)),
        ],
        compiler_params=PARAMS,
        cost_estimate=cost(1),
        name="last",
    )(base, other_received)
    return state.reshape(1, SPEC, LAYERS, COLS)


def solution(mesh):
    return jax.shard_map(
        local,
        mesh=mesh,
        in_specs=(
            P("group", None, None, "tile"),
            P(None, "tile"),
            P(None, "tile"),
            P(None, "tile"),
            P(),
            P(),
            P(),
            P(),
            P(),
            P(),
            P(),
        ),
        out_specs=P("group", None, None, "tile"),
        check_vma=False,
    )
```

```python
import jax
import jax.numpy as jnp
from jax import lax
from jax.experimental import pallas as pl
from jax.experimental.pallas import tpu as pltpu
from jax.sharding import PartitionSpec as P

SPEC = 220
REAC = 500
PHOT = 64
LAYERS = 8
COLS = 128
ADV_STEPS = 4
ITER_NIGHT = 2
ITER_DAY = 4

HALF = LAYERS // 2
ROWS = SPEC * LAYERS
SPAD = 224
KDIM = 256
RPAD = 512
CELLS = HALF * COLS
PIECES = 7
PACKED = PIECES * COLS
PARTS = 2
SENDS = 1
CHUNK = 256
EDGE = 4
DARK = -1024.0

MIDDLE = (4, 3, 5, 2, 6, 1, 7, 0)
INNER = (2, 1, 3, 0)
ORDER = [z * 16 + x * 4 + y for z in MIDDLE for x in INNER for y in INNER]

VMEM = pl.BlockSpec(memory_space=pltpu.VMEM)
HBM = pl.BlockSpec(memory_space=pltpu.HBM)
PARAMS = pltpu.CompilerParams(vmem_limit_bytes=24 * 1024 * 1024)


def high_low(value):
    high = value.astype(jnp.bfloat16)
    return high, (value - high.astype(jnp.float32)).astype(jnp.bfloat16)


def dot(a, b):
    return jnp.dot(a, b, preferred_element_type=jnp.float32)


def pick(table, index):
    out = jnp.zeros_like(index)
    for at, value in enumerate(table):
        out = jnp.where(index == at, value, out)
    return out


def tile_at(place):
    return pick(MIDDLE, place // 16) * 16 + pick(INNER, place // 4 % 4) * 4 + pick(INNER, place % 4)


def place_of(tile):
    middle = [MIDDLE.index(z) for z in range(8)]
    inner = [INNER.index(z) for z in range(4)]
    return pick(middle, tile // 16) * 16 + pick(inner, tile // 4 % 4) * 4 + pick(inner, tile % 4)


def prepare_kernel(table, weights, gather, turning):
    spare = pl.ds(RPAD - COLS, COLS)
    weights[:, spare] = jnp.zeros((3 * SPAD, COLS), jnp.bfloat16)
    turning[:, spare] = jnp.zeros((KDIM, COLS), jnp.float32)
    row_of = [table[row : row + 1, :] for row in range(8)]

    used = pl.ds(0, REAC)
    species = lax.broadcasted_iota(jnp.int32, (SPAD, REAC), 0).astype(jnp.float32)
    thermal = lax.broadcasted_iota(jnp.int32, (1, REAC), 1) >= PHOT
    second = jnp.where(thermal, row_of[1], -1.0)
    consuming = jnp.where(species == row_of[0], 1.0, 0.0) + jnp.where(
        species == second, 1.0, 0.0
    )
    producing = jnp.where(species == row_of[2], row_of[4], 0.0) + jnp.where(
        species == row_of[3], row_of[5], 0.0
    )
    producing_high, producing_low = high_low(producing)
    weights[pl.ds(0, SPAD), used] = consuming.astype(jnp.bfloat16)
    weights[pl.ds(SPAD, SPAD), used] = producing_high
    weights[pl.ds(2 * SPAD, SPAD), used] = producing_low

    speed = lax.log2(row_of[6])
    speed_high = speed.astype(jnp.bfloat16).astype(jnp.float32)
    speed_mid = (speed - speed_high).astype(jnp.bfloat16).astype(jnp.float32)
    speed_low = speed - speed_high - speed_mid
    barrier = jnp.where(thermal, row_of[7], 0.0)
    barrier_high = barrier.astype(jnp.bfloat16).astype(jnp.float32)
    barrier_low = barrier - barrier_high
    photo = jnp.where(thermal, 0.0, 1.0)
    row = lax.broadcasted_iota(jnp.int32, (KDIM - SPAD, REAC), 0)
    extra = jnp.zeros((KDIM - SPAD, REAC), jnp.float32)
    for place, value in enumerate(
        (barrier_high, barrier_low, speed_high, speed_mid, speed_low, photo)
    ):
        extra = jnp.where(row == place, value, extra)
    turning[pl.ds(0, SPAD), used] = consuming
    turning[pl.ds(SPAD, KDIM - SPAD), used] = extra
    gather[...] = jnp.transpose(turning[...]).astype(jnp.bfloat16)


def choose_kernel(lookup, choose):
    tile = lax.axis_index("tile")
    lane = lax.broadcasted_iota(jnp.int32, (COLS, COLS), 1)
    column = jnp.sum(jnp.where(lane == tile, lookup[...], 0), axis=1, keepdims=True)
    chosen = jnp.where(lane == column - tile * COLS, 1.0, 0.0)
    ordered = jnp.where(lane == tile_at(lax.broadcasted_iota(jnp.int32, (COLS, COLS), 0)), 1.0, 0.0)
    choose[...] = dot(ordered.astype(jnp.bfloat16), chosen.astype(jnp.bfloat16)).astype(jnp.bfloat16)


def chemistry_kernel(
    own,
    swapped,
    marker,
    choose,
    heat,
    light,
    weights,
    gather,
    send,
    tendency,
    logs,
    start,
    now,
    stack,
    parts,
    packed,
    sems,
):
    group, tile = lax.axis_index("group"), lax.axis_index("tile")

    lit = jnp.max(marker[pl.ds(tile, 1), :])
    sweeps = jnp.where(lit > 0, ITER_DAY, ITER_NIGHT)
    row = lax.broadcasted_iota(jnp.int32, (KDIM - SPAD, COLS), 0)
    for layer in range(HALF):
        warmth = heat[pl.ds(group * HALF + layer, 1), :]
        flux = light[pl.ds(group * HALF + layer, 1), :]
        inverse = (1.0 / 250.0 - 1.0 / warmth) * 1.4426950408889634
        flux = jnp.where(lit > 0, lax.log2(flux), DARK)
        term = jnp.where(row < 2, inverse, 0.0)
        term = jnp.where((row >= 2) & (row < 5), 1.0, term)
        term = jnp.where(row == 5, flux, term)
        term_high, term_low = high_low(term)
        logs[SPAD:KDIM, pl.ds(layer * COLS, COLS)] = term_high
        logs[KDIM + SPAD :, pl.ds(layer * COLS, COLS)] = term_low
    for core, amounts in enumerate((swapped, own)):

        @pl.when(group == core)
        def _():
            for layer in range(HALF):
                begin = amounts[pl.ds(core * HALF + layer, SPEC, stride=LAYERS), :]
                start[0:SPEC, pl.ds(layer * COLS, COLS)] = begin

    start[SPEC:SPAD, :] = jnp.ones((SPAD - SPEC, CELLS), jnp.float32)
    now[...] = start[...]
    chunks = [pl.ds(at, CHUNK) for at in range(0, CELLS, CHUNK)]

    def sweep():
        for cells in chunks:
            log_high, log_low = high_low(lax.log2(now[:, cells]))
            logs[0:SPAD, cells] = log_high
            logs[KDIM : KDIM + SPAD, cells] = log_low
        for cells in chunks:
            rate = jnp.exp2(
                dot(gather[...], logs[0:KDIM, cells]) + dot(gather[...], logs[KDIM:, cells])
            )
            high, low = high_low(rate)
            both = dot(weights[0 : 2 * SPAD], high) + dot(weights[0 : 2 * SPAD], low)
            gain = both[SPAD:] + dot(weights[2 * SPAD :], high)
            concen = now[:, cells]
            now[:, cells] = concen * (start[:, cells] + gain) / (concen + both[:SPAD])

    @pl.loop(0, sweeps // 2)
    def _(_):
        sweep()
        sweep()

    for layer in range(HALF):
        cells = pl.ds(layer * COLS, COLS)
        stack[pl.ds(layer, SPEC, stride=HALF), :] = now[0:SPEC, cells]
    stack[HALF * SPEC :, :] = jnp.zeros((PACKED - HALF * SPEC, COLS), jnp.float32)
    for piece in range(PIECES):
        rest = jnp.transpose(stack[pl.ds(piece * COLS, COLS), :])
        for part in range(PARTS):
            rounded = rest.astype(jnp.bfloat16)
            rest = rest - rounded.astype(jnp.float32)
            parts[pl.ds(part * COLS, COLS), pl.ds(piece * COLS, COLS)] = rounded
    copies = []
    owners = COLS // SENDS
    for part in range(SENDS):
        turned = dot(
            jnp.concatenate([choose[part * owners : (part + 1) * owners, :]] * PARTS, axis=1),
            parts[...],
        )
        for piece in range(PIECES):
            packed[pl.ds(part * owners * PIECES + piece, owners, stride=PIECES), :] = turned[
                :, piece * COLS : (piece + 1) * COLS
            ]
        rows = pl.ds(part * owners * PIECES, owners * PIECES)
        copies.append(pltpu.make_async_copy(packed.at[rows], send.at[rows], sems.at[part]))
        copies[part].start()
    for layer in range(HALF):
        cells = pl.ds(layer * COLS, COLS)
        tendency[pl.ds(layer * SPAD, SPAD), :] = now[:, cells] - start[:, cells]
    for copy in copies:
        copy.wait()


def across(a, b):
    return lax.dot_general(a, b, (((1,), (1,)), ((), ())), preferred_element_type=jnp.float32)


def edge_kernel(tracers, wind, far, near, padded):
    odd = lax.axis_index("tile") % 2 == 1
    row = lax.broadcasted_iota(jnp.int32, (2 * EDGE, COLS), 0)
    column = lax.broadcasted_iota(jnp.int32, (2 * EDGE, COLS), 1)
    choose = jnp.where(column == (row + COLS - EDGE) % COLS, 1.0, 0.0).astype(jnp.bfloat16)
    for layer in range(LAYERS):
        padded[layer, SPEC - 4 :, :] = jnp.zeros((KDIM - SPEC + 4, COLS), jnp.float32)
        padded[layer, 0:SPEC, :] = tracers[pl.ds(layer, SPEC, stride=LAYERS), :]
        padded[layer, SPEC : SPEC + 1, :] = wind[layer : layer + 1, :]
    for layer in range(LAYERS):
        high, low = high_low(padded[layer])
        picked = across(choose, high) + across(choose, low)
        to_high, to_low = picked[:EDGE], picked[EDGE:]
        far[pl.ds(layer * EDGE, EDGE), :] = jnp.where(odd, to_high, to_low)
        near[pl.ds(layer * EDGE, EDGE), :] = jnp.where(odd, to_low, to_high)


def advect(tracers, wind, far, near, own_tend, other_tend, state, after):
    tile = lax.axis_index("tile")
    odd = tile % 2 == 1
    side = EDGE * LAYERS
    low_there = jnp.where(tile > 0, 1.0, 0.0)
    high_there = jnp.where(tile < COLS - 1, 1.0, 0.0)
    beside = jnp.concatenate(
        [
            jnp.where(odd, near[...], far[...]) * low_there,
            jnp.where(odd, far[...], near[...]) * high_there,
            jnp.zeros((COLS - 2 * side, KDIM), jnp.float32),
        ],
        axis=0,
    )
    beside = jnp.transpose(beside)
    wind_row = jnp.broadcast_to(beside[SPEC : SPEC + 1, :], (LAYERS, COLS))
    layer_of = lax.broadcasted_iota(jnp.int32, (LAYERS, COLS), 0)
    right_half = lax.broadcasted_iota(jnp.int32, (LAYERS, COLS), 1) >= COLS // 2
    wind_side = jnp.zeros((LAYERS, COLS), jnp.float32)
    for layer in range(LAYERS):
        low = pltpu.roll(wind_row, COLS - EDGE - EDGE * layer, 1)
        high = pltpu.roll(wind_row, COLS - side - EDGE * layer, 1)
        wind_side = jnp.where(layer_of == layer, jnp.where(right_half, low, high), wind_side)

    lane = lax.broadcasted_iota(jnp.int32, (LAYERS, COLS), 1)
    lowest, highest = lane == 0, lane == COLS - 1

    def left(pair):
        up = [pltpu.roll(v, 1, 1) for v in pair]
        return jnp.where(lowest, up[1], up[0]), jnp.where(lowest, up[0], up[1])

    def right(pair):
        down = [pltpu.roll(v, COLS - 1, 1) for v in pair]
        return jnp.where(highest, down[1], down[0]), jnp.where(highest, down[0], down[1])

    factors = [
        (0.5 * c * (1.0 + c), 1.0 - c * c, 0.5 * c * (c - 1.0)) for c in (wind[...], wind_side)
    ]
    one = jnp.ones((LAYERS, COLS), jnp.float32)
    band = {0: (one, one)}
    for _ in range(ADV_STEPS):
        lefts = {d: left(pair) for d, pair in band.items()}
        rights = {d: right(pair) for d, pair in band.items()}
        reach = max(band) + 1
        fresh = {}
        for d in range(-reach, reach + 1):
            total = [0.0, 0.0]
            for source, factor in ((lefts.get(d + 1), 0), (band.get(d), 1), (rights.get(d - 1), 2)):
                if source is not None:
                    total = [t + factors[i][factor] * source[i] for i, t in enumerate(total)]
            fresh[d] = tuple(total)
        band = fresh

    rows = lax.broadcasted_iota(jnp.int32, (KDIM, COLS), 0)
    extra = rows - COLS
    edge = extra % EDGE
    place = jnp.where(rows < COLS, rows, jnp.where(extra < side, edge - EDGE, edge + COLS))
    offset = place - lax.broadcasted_iota(jnp.int32, (KDIM, COLS), 1)
    beside_high, beside_low = high_low(beside[:SPAD])
    for layer in range(LAYERS):
        here = (rows < COLS) | (extra % side // EDGE == layer)
        matrix = jnp.zeros((KDIM, COLS), jnp.float32)
        for d, (weight, _) in band.items():
            matrix = jnp.where(offset == d, weight[layer : layer + 1, :], matrix)
        matrix_high, matrix_low = high_low(jnp.where(here, matrix, 0.0))
        main = jnp.concatenate(
            [
                tracers[pl.ds(layer, SPEC, stride=LAYERS), :],
                jnp.zeros((SPAD - SPEC, COLS), jnp.float32),
            ],
            axis=0,
        )
        main_high, main_low = high_low(main)
        high = jnp.concatenate([main_high, beside_high], axis=1)
        low = jnp.concatenate([main_low, beside_low], axis=1)
        moved = dot(high, matrix_high) + dot(low, matrix_high) + dot(high, matrix_low)
        tend = own_tend if layer < HALF else other_tend
        state[pl.ds(layer, SPEC, stride=LAYERS), :] = (
            moved[:SPEC] + tend[pl.ds(layer % HALF * SPAD, SPEC), :]
        )
        after(layer)


def unpack(block, stack, state, begin, after):
    order = place_of(lax.broadcasted_iota(jnp.int32, (COLS, COLS), 1))
    for piece in range(PIECES):
        turned = jnp.transpose(block[pl.ds(piece, COLS, stride=PIECES), :])
        stack[pl.ds(piece * COLS, COLS), :] = jnp.take_along_axis(turned, order, axis=1)
        first, count = slab(piece)
        for layer in range(HALF):
            state[pl.ds(first * LAYERS + begin + layer, count, stride=LAYERS), :] = stack[
                pl.ds(piece * COLS + layer, count, stride=HALF), :
            ]
        after(piece)


def slab(piece):
    first = piece * COLS // HALF
    return first, min(COLS // HALF, SPEC - first)


def to_state(source, state, sem, first, count, begin):
    species, layers = pl.ds(first, count), pl.ds(begin, HALF)
    return pltpu.make_async_copy(
        source.reshape(SPEC, LAYERS, COLS).at[species, layers, :],
        state.reshape(SPEC, LAYERS, COLS).at[species, layers, :],
        sem,
    )


def first_kernel(
    tracers,
    wind,
    far,
    near,
    own_tend,
    other_tend,
    own,
    state,
    here,
    stack,
    sems,
):
    @pl.when(lax.axis_index("group") == 0)
    def _():
        def copy(layer):
            part = layer // HALF
            return to_state(here, state, sems.at[part], 0, SPEC, part * HALF)

        def after(layer):
            if layer % HALF == HALF - 1:
                copy(layer).start()

        advect(tracers, wind, far, near, own_tend, other_tend, here, after)
        for layer in (0, HALF):
            copy(layer).wait()

    @pl.when(lax.axis_index("group") == 1)
    def _():
        copies = [
            to_state(here, state, sems.at[piece], *slab(piece), HALF) for piece in range(PIECES)
        ]
        unpack(own, stack, here, HALF, lambda piece: copies[piece].start())
        for copy in copies:
            copy.wait()


def last_kernel(base, other, state, here, stack, sems):
    @pl.when(lax.axis_index("group") == 1)
    def _():
        copies = [
            to_state(here, state, sems.at[piece], *slab(piece), 0) for piece in range(PIECES)
        ]
        unpack(other, stack, here, 0, lambda piece: copies[piece].start())
        for copy in copies:
            copy.wait()


def cost(microseconds):
    return pl.CostEstimate(
        flops=int(microseconds * 1e9), bytes_accessed=int(microseconds * 2e6), transcendentals=0
    )


def bf16(*shape):
    return jax.ShapeDtypeStruct(shape, jnp.bfloat16)


def f32(*shape):
    return jax.ShapeDtypeStruct(shape, jnp.float32)


def exchanged(tiles):
    return [pair for i in tiles for pair in ((i, i + 1), (i + 1, i))]


def local(
    species_amounts,
    air_warmth_kelvin,
    sunlight_strength,
    wind_stability_numbers,
    illuminated_marker,
    position_vertical_lookup,
    speed_constants,
    barrier_kelvins,
    consumed_species,
    outcome_species,
    outcome_fractions,
):
    amounts = species_amounts.reshape(ROWS, COLS)
    swap = [(0, 1), (1, 0)]
    swapped = lax.ppermute(amounts, "group", swap)

    table = jnp.concatenate(
        [
            consumed_species.astype(jnp.float32),
            outcome_species.astype(jnp.float32),
            outcome_fractions,
            speed_constants[None],
            barrier_kelvins[None],
        ]
    )
    weights, gather = pl.pallas_call(
        prepare_kernel,
        out_shape=(bf16(3 * SPAD, RPAD), bf16(RPAD, KDIM)),
        in_specs=[VMEM],
        out_specs=(VMEM, VMEM),
        scratch_shapes=[pltpu.VMEM((KDIM, RPAD), jnp.float32)],
        compiler_params=PARAMS,
        cost_estimate=cost(1),
        name="prepare",
    )(table)
    choose = pl.pallas_call(
        choose_kernel,
        out_shape=bf16(COLS, COLS),
        in_specs=[VMEM],
        out_specs=VMEM,
        compiler_params=PARAMS,
        cost_estimate=cost(1),
        name="choose",
    )(position_vertical_lookup.reshape(COLS, COLS))
    send, tendency = pl.pallas_call(
        chemistry_kernel,
        out_shape=(f32(PACKED, COLS), f32(HALF * SPAD, COLS)),
        in_specs=[VMEM] * 8,
        out_specs=(HBM, VMEM),
        scratch_shapes=[
            pltpu.VMEM((2 * KDIM, CELLS), jnp.bfloat16),
            pltpu.VMEM((SPAD, CELLS), jnp.float32),
            pltpu.VMEM((SPAD, CELLS), jnp.float32),
            pltpu.VMEM((PACKED, COLS), jnp.float32),
            pltpu.VMEM((PARTS * COLS, PACKED), jnp.bfloat16),
            pltpu.VMEM((PACKED, COLS), jnp.float32),
            pltpu.SemaphoreType.DMA((SENDS,)),
        ],
        compiler_params=PARAMS,
        cost_estimate=cost(6),
        name="chemistry",
    )(
            amounts,
        swapped,
        illuminated_marker.reshape(COLS, COLS),
        choose,
        air_warmth_kelvin,
        sunlight_strength,
        weights,
        gather,
    )
    received = lax.all_to_all(
        send.reshape(COLS, 1, PACKED),
        "tile",
        split_axis=0,
        concat_axis=0,
        axis_index_groups=[ORDER],
        tiled=True,
    )

    far, near = pl.pallas_call(
        edge_kernel,
        out_shape=(f32(EDGE * LAYERS, KDIM), f32(EDGE * LAYERS, KDIM)),
        in_specs=[VMEM, VMEM],
        out_specs=(VMEM, VMEM),
        scratch_shapes=[pltpu.VMEM((LAYERS, KDIM, COLS), jnp.float32)],
        compiler_params=PARAMS,
        cost_estimate=cost(1),
        name="edges",
    )(amounts, wind_stability_numbers)
    count = lax.axis_size("tile")
    both = ("group", "tile")
    far = lax.ppermute(far, both, exchanged(range(1, count - 1, 2)))
    near = lax.ppermute(near, both, exchanged(range(0, count, 2)))
    other_tendency = lax.ppermute(tendency, "group", swap)
    received, other_tendency = lax.optimization_barrier((received, other_tendency))
    received = received.reshape(PACKED, COLS)
    other_received = lax.ppermute(received, "group", swap)
    base = pl.pallas_call(
        first_kernel,
        out_shape=f32(ROWS, COLS),
        in_specs=[VMEM] * 7,
        out_specs=HBM,
        scratch_shapes=[
            pltpu.VMEM((ROWS, COLS), jnp.float32),
            pltpu.VMEM((PACKED, COLS), jnp.float32),
            pltpu.SemaphoreType.DMA((PIECES,)),
        ],
        compiler_params=PARAMS,
        cost_estimate=cost(20),
        name="first",
    )(
            amounts,
        wind_stability_numbers,
        far,
        near,
        tendency,
        other_tendency,
        received,
    )
    state = pl.pallas_call(
        last_kernel,
        out_shape=f32(ROWS, COLS),
        in_specs=[HBM, VMEM],
        out_specs=HBM,
        input_output_aliases={0: 0},
        scratch_shapes=[
            pltpu.VMEM((ROWS, COLS), jnp.float32),
            pltpu.VMEM((PACKED, COLS), jnp.float32),
            pltpu.SemaphoreType.DMA((PIECES,)),
        ],
        compiler_params=PARAMS,
        cost_estimate=cost(1),
        name="last",
    )(base, other_received)
    return state.reshape(1, SPEC, LAYERS, COLS)


def solution(mesh):
    return jax.shard_map(
        local,
        mesh=mesh,
        in_specs=(
            P("group", None, None, "tile"),
            P(None, "tile"),
            P(None, "tile"),
            P(None, "tile"),
            P(),
            P(),
            P(),
            P(),
            P(),
            P(),
            P(),
        ),
        out_specs=P("group", None, None, "tile"),
        check_vma=False,
    )
```
